256 devices in a mesh: section: 2 (over x_hi), dp: 128 (over y, z, x_lo, core).
Axes of the slice: x: 4 (x_hi: 2, x_lo: 2; x = x_hi * 2 + x_lo), y: 4, z: 8, core: 2. Of those that a mesh axis runs over, the one named last changes fastest.
Arguments:
- inputs: bfloat16 [2, 2, 16384, 1280], P('section', None, 'dp'), may hold values from -24 to 24
- weights: bfloat16 [2, 1280, 1280], P('section'), may hold values from -0.15625 to 0.15625
- gains: float32 [2, 1280], P('section'), may hold values from 0.1 to 1.9
- timesteps: int32 [2, 16], replicated, may hold values from 0 to 999
- text_pooled: bfloat16 [2, 16, 1280], replicated, may hold values from -6 to 6
Outputs:
- section_outputs: bfloat16 [2, 2, 16384, 1280], P('section', None, 'dp')
- weight_grad: float32 [2, 1280, 1280], P('section', 'dp')
The draws below stay inside these ranges and needn't reach their ends.
All inputs are finite; a program needn't handle non-finite values.
Results may differ from the reference program's by a relative error of at most 0.0047.
Values may be sent and summed in bfloat16 or wider, within the bound.
No kernel may reach another device: no remote copies, remote signals or barrier semaphores. Data moves between devices by JAX's collectives and lax.ppermute only.
A program may use at most 64 MiB of HBM per device.

```python
import math
import jax
import jax.numpy as jnp
from jax import lax

C = 1280
PIX = 1024
MICRO = 2
TOKENS = 16384
LAT_MB = 16


def place_ends(drawn, rng, smallest, high):
    index_at = [jax.random.randint(jax.random.fold_in(rng, axis), (), 0, length) for axis, length in enumerate(drawn.shape)]
    longest = drawn.shape.index(max(drawn.shape))
    next_to = index_at[:longest] + [(index_at[longest] + 1) % drawn.shape[longest]] + index_at[longest + 1:]
    return drawn.at[tuple(index_at)].set(smallest).at[tuple(next_to)].set(high)


def spiked(values, own_key, source, target, blocks, factor):
    owner, partner = [(jnp.arange(values.shape[dim]) // (values.shape[dim] // blocks)).reshape([-1 if axis == dim else 1 for axis in range(values.ndim)]) for dim in (source, target)]
    chosen = jax.random.permutation(own_key, blocks)[partner]
    strong = (owner == chosen) | (owner == (partner + blocks // 2) % blocks)
    return jnp.where(strong, factor * values, values)


def block_scale(key, extent, split, low, high):
    loudness, own = 1.0, jax.random.fold_in(key, 6)
    for axis_at, shards_of in split:
        steps = jnp.exp(jax.random.uniform(jax.random.fold_in(own, axis_at), (shards_of,), jnp.float32, low / len(split), high / len(split)))
        loudness = loudness * jnp.repeat(steps, extent[axis_at] // shards_of).reshape([-1 if axis == axis_at else 1 for axis in range(len(extent))])
    return loudness


def gaussian(own_key, dims, scale, reach, shards=(), held_as=jnp.bfloat16):
    loudness = block_scale(own_key, dims, shards, -0.22, 0.18) if shards else 1.0
    values = jax.random.normal(own_key, dims, jnp.float32) * scale * loudness
    return jnp.minimum(jnp.maximum(values, -reach), reach).astype(held_as)


def bell_draw_with(own_key, dims, scale, most, pieces, heavy, kind=jnp.bfloat16):
    drawn = scale * jax.random.normal(own_key, dims, jnp.float32)
    if pieces:
        drawn = drawn * block_scale(own_key, dims, pieces, -0.22, 0.18)
    return jnp.clip(spiked(drawn, jax.random.fold_in(own_key, 3), *heavy), -most, most).astype(kind)


def setup_inputs(seed: int = 0) -> dict:
    key_of = jax.random.split(jax.random.key(seed), 6)
    return {
        "inputs": bell_draw_with(key_of[0], (2, MICRO, TOKENS, C), 1.0, 24.0, ((0, 2), (2, 128)), (2, 3, 128, 5.5)),
        "weights": gaussian(key_of[1], (2, C, C), C ** -0.5, 0.15625, ((0, 2),)),
        "gains": jnp.clip(1.0 + 0.18 * jax.random.normal(key_of[2], (2, C), jnp.float32), 0.1, 1.9),
        "timesteps": place_ends(jax.random.randint(key_of[3], (MICRO, LAT_MB), 0, 1000), jax.random.fold_in(key_of[3], 1), 0, 999).astype(jnp.int32),
        "text_pooled": gaussian(key_of[4], (MICRO, LAT_MB, C), 1.0, 6.0),
    }


def latent_condition(steps_row, pooled_row):
    width = pooled_row.shape[-1]
    half_width = width // 2
    frequency = jnp.exp(-math.log(10000.0) * jnp.arange(half_width, dtype=jnp.float32) / half_width)
    angles = steps_row.astype(jnp.float32)[:, None] * frequency[None, :]
    return jnp.concatenate([jnp.cos(angles), jnp.sin(angles)], axis=1) + pooled_row.astype(jnp.float32)

def forward_layer(hidden, condition, weight, gain):
    shifted = hidden.astype(jnp.float32) + condition
    inverse = lax.rsqrt(lax.optimization_barrier(jnp.mean(shifted * shifted, axis=-1, keepdims=True)) + 1e-05)
    normed = shifted * inverse * gain.astype(jnp.float32)
    active = jax.nn.silu(normed).astype(jnp.bfloat16)
    result = hidden.astype(jnp.float32) + jnp.dot(active, weight, preferred_element_type=jnp.float32)
    return (result, (shifted, inverse, normed, active))

def backward_layer(upstream, saved, weight, gain):
    shifted, inverse, normed, active = saved
    through = lax.dot_general(upstream, weight, (((1,), (1,)), ((), ())), preferred_element_type=jnp.float32)
    sigma = jax.nn.sigmoid(normed)
    scaled = through * sigma * (1.0 + normed * (1.0 - sigma)) * gain.astype(jnp.float32)
    inner = lax.optimization_barrier(jnp.mean(scaled * shifted, axis=-1, keepdims=True))
    return (upstream.astype(jnp.float32) + inverse * scaled - shifted * inverse ** 3 * inner).astype(jnp.bfloat16)

def weight_term(active_rows, upstream_rows):
    return lax.dot_general(active_rows, upstream_rows, (((0,), (0,)), ((), ())), preferred_element_type=jnp.float32)

def reference(inputs, weights, gains, timesteps, text_pooled):
    loss_scale = math.sqrt(MICRO * TOKENS)
    grad_down = jnp.zeros((C, C), jnp.float32)
    grad_up = jnp.zeros((C, C), jnp.float32)
    down_list = []
    up_list = []
    for number in range(MICRO):
        condition = jnp.repeat(latent_condition(timesteps[number], text_pooled[number]), PIX, axis=0)
        first_out, first_saved = forward_layer(inputs[0, number], condition, weights[0], gains[0])
        down_rows = first_out.astype(jnp.bfloat16)
        second_out, second_saved = forward_layer(down_rows, condition, weights[1], gains[1])
        target_cot = ((second_out - inputs[1, number].astype(jnp.float32)) / loss_scale).astype(jnp.bfloat16)
        back_rows = backward_layer(target_cot, second_saved, weights[1], gains[1])
        grad_up = grad_up + weight_term(second_saved[3], target_cot)
        grad_down = grad_down + weight_term(first_saved[3], back_rows)
        down_list.append(down_rows)
        up_list.append(second_out.astype(jnp.bfloat16))
    section_outputs = jnp.stack([jnp.stack(down_list), jnp.stack(up_list)])
    return (section_outputs, jnp.stack([grad_down, grad_up]))
```

```python
import math

import jax
import jax.numpy as jnp
from jax import lax
from jax.sharding import Mesh, PartitionSpec as P

PIX = 1024
MICRO = 2
TOK_DEV = 128
DP = ("y", "z", "x", "core")
GROUP = ("x", "core")
LANES = 128


def latent_condition(step, pooled_row):
    width = pooled_row.shape[-1]
    half_width = width // 2
    frequency = jnp.exp(-math.log(10000.0) * jnp.arange(half_width, dtype=jnp.float32) / half_width)
    angles = step.astype(jnp.float32) * frequency
    return jnp.concatenate([jnp.cos(angles), jnp.sin(angles)]) + pooled_row.astype(jnp.float32)


def forward_layer(hidden, condition, weight, gain):
    shifted = hidden.astype(jnp.float32) + condition
    inverse = lax.rsqrt(jnp.mean(shifted * shifted, axis=-1, keepdims=True) + 1e-05)
    normed = shifted * inverse * gain
    active = jax.nn.silu(normed).astype(jnp.bfloat16)
    result = hidden.astype(jnp.float32) + jnp.dot(
        active, weight, preferred_element_type=jnp.float32
    )
    return (result, (shifted, inverse, normed, active))


def backward_layer(upstream, saved, weight, gain):
    shifted, inverse, normed, active = saved
    through = lax.dot_general(
        upstream, weight, (((1,), (1,)), ((), ())), preferred_element_type=jnp.float32
    )
    sigma = jax.nn.sigmoid(normed)
    scaled = through * sigma * (1.0 + normed * (1.0 - sigma)) * gain
    inner = jnp.mean(scaled * shifted, axis=-1, keepdims=True)
    return (
        upstream.astype(jnp.float32) + inverse * scaled - shifted * inverse**3 * inner
    ).astype(jnp.bfloat16)


def swap(block, axis):
    return lax.ppermute(block, axis, [(0, 1), (1, 0)])


def local(inputs, weights, gains, timesteps, text_pooled):
    local_rows = inputs[0]
    weight = weights[0]
    gain = gains[0]
    width = weight.shape[0]
    quarter = width // 4
    down_section = lax.axis_index("section") == 0
    loss_scale = math.sqrt(MICRO * TOK_DEV * LANES)
    latent = lax.axis_index(DP) * TOK_DEV // PIX
    conditions = [
        latent_condition(timesteps[number, latent], text_pooled[number, latent])
        for number in range(MICRO)
    ]
    first_out, first_active, received = [], [], []
    for number in range(MICRO):
        out, saved = forward_layer(local_rows[number], conditions[number], weight, gain)
        first_out.append(out.astype(jnp.bfloat16))
        first_active.append(saved[3])
        received.append(lax.ppermute(first_out[-1], "section", [(0, 1)]))
    second_out, second_active, cots, backs = [], [], [], []
    for number in range(MICRO):
        out, saved = forward_layer(received[number], conditions[number], weight, gain)
        second_out.append(out.astype(jnp.bfloat16))
        second_active.append(saved[3])
        cot = ((out - local_rows[number].astype(jnp.float32)) / loss_scale).astype(jnp.bfloat16)
        cots.append(cot)
        backs.append(backward_layer(cot, saved, weight, gain))
    results = jnp.where(down_section, jnp.stack(first_out), jnp.stack(second_out))
    active = jnp.where(down_section, jnp.concatenate(first_active), jnp.concatenate(second_active))
    far = swap(active, "x")
    near = swap(active, "core")
    far_core = swap(far, "core")

    upstream = jnp.stack([jnp.concatenate(backs), jnp.concatenate(cots)])
    pieces = jnp.transpose(upstream.reshape(2, -1, 4, quarter), (0, 2, 1, 3))
    pieces = pieces.reshape(8, -1, quarter)
    arrived = lax.all_to_all(pieces, ("section",) + GROUP, 0, 0, tiled=True)[4:]
    x_at, core_at = lax.axis_index("x"), lax.axis_index("core")
    partial = jnp.zeros((width, quarter), jnp.float32)
    for block, x_off, core_off in ((active, 0, 0), (near, 0, 1), (far, 1, 0), (far_core, 1, 1)):
        source = ((x_at + x_off) % 2) * 2 + (core_at + core_off) % 2
        rows = lax.dynamic_index_in_dim(arrived, source, 0, keepdims=False)
        partial += lax.dot_general(
            block, rows, (((0,), (0,)), ((), ())), preferred_element_type=jnp.float32
        )
    shares = partial.astype(jnp.bfloat16).reshape(LANES, width // LANES, quarter)
    shares = lax.all_to_all(shares, DP, 0, 0, tiled=True)
    shares = shares.reshape(LANES // 4, 4, width // LANES, quarter).astype(jnp.float32)
    summed = jnp.sum(shares, axis=0)
    gradient = jnp.transpose(summed, (1, 0, 2)).reshape(width // LANES, width)
    return (results[None], gradient[None])


def solution(mesh):
    fine = Mesh(mesh.devices.reshape(2, 4, 8, 2, 2), ("section",) + DP)
    return jax.shard_map(
        local,
        mesh=fine,
        in_specs=(
            P("section", None, DP, None),
            P("section", None, None),
            P("section", None),
            P(),
            P(),
        ),
        out_specs=(P("section", None, DP, None), P("section", DP, None)),
        check_vma=False,
    )
```

```python
import functools
import math

import jax
import jax.numpy as jnp
from jax import lax
from jax.experimental import pallas as pl
from jax.experimental.pallas import tpu as pltpu
from jax.sharding import Mesh, PartitionSpec as P

PIX = 1024
MICRO = 2
ROWS = 128
LANES = 128
C = 1280
DP = ("yh", "yl", "z", "x", "core")
GROUP = ("yl", "core")
PIECE = 320
SHARE = 32
PARAMS = pltpu.CompilerParams(vmem_limit_bytes=40 * 1024 * 1024)
VMEM = pl.BlockSpec(memory_space=pltpu.VMEM)
SMEM = pl.BlockSpec(memory_space=pltpu.SMEM)


def condition_row(steps_ref, text_ref, number):
    latent = lax.axis_index(DP) * ROWS // PIX
    step = steps_ref[number, latent].astype(jnp.float32)
    lane = lax.broadcasted_iota(jnp.int32, (1, C), 1)
    index = jnp.where(lane < C // 2, lane, lane - C // 2).astype(jnp.float32)
    angle = step * jnp.exp(-math.log(10000.0) * index / (C // 2))
    waves = jnp.where(lane < C // 2, jnp.cos(angle), jnp.sin(angle))
    text = text_ref[number].astype(jnp.float32)
    mine = lax.broadcasted_iota(jnp.int32, text.shape, 0) == latent
    return waves + jnp.sum(jnp.where(mine, text, 0.0), axis=0, keepdims=True)


def normed_rows(hidden, condition, gain):
    shifted = hidden + condition
    inverse = lax.rsqrt(jnp.mean(shifted * shifted, axis=-1, keepdims=True) + 1e-05)
    normed = shifted * inverse * gain
    sigma = 1.0 / (1.0 + jnp.exp(-normed))
    return shifted, inverse, normed, sigma


def down_kernel(number, steps_ref, rows_ref, weight_ref, gain_ref, text_ref, sent_ref, active_ref):
    hidden = rows_ref[0, number].astype(jnp.float32)
    condition = condition_row(steps_ref, text_ref, number)
    _, _, normed, sigma = normed_rows(hidden, condition, gain_ref[...])
    active = (normed * sigma).astype(jnp.bfloat16)
    active_ref[...] = active
    result = hidden + jnp.dot(active, weight_ref[0], preferred_element_type=jnp.float32)
    sent_ref[...] = result.astype(jnp.bfloat16)


def store_pieces(pieces_ref, first, values):
    half = ROWS // 2
    low = lax.broadcasted_iota(jnp.int32, (half, 128), 1) < 64
    rounded = values.astype(jnp.bfloat16)
    for quarter in range(4):
        slot = first + quarter
        pieces_ref[slot, :ROWS] = rounded[:, 256 * quarter : 256 * quarter + 128]
        pieces_ref[slot, ROWS : 2 * ROWS] = rounded[:, 256 * quarter + 128 : 256 * quarter + 256]
        at = 1024 + 128 * (quarter // 2)
        block = values[:, at : at + 128]
        turned = pltpu.roll(block, 64, 1)
        top, bottom = (block, turned) if quarter % 2 == 0 else (turned, block)
        pieces_ref[slot, 2 * ROWS :] = jnp.where(low, top[:half], bottom[half:]).astype(
            jnp.bfloat16
        )


def up_kernel(
    number, steps_ref, arrived_ref, rows_ref, weight_ref, gain_ref, text_ref, sent_ref,
    first_active_ref, out_ref, active_ref, pieces_ref,
):
    down = lax.axis_index("section") == 0
    gain = gain_ref[...]
    hidden = arrived_ref[...].astype(jnp.float32)
    condition = condition_row(steps_ref, text_ref, number)
    shifted, inverse, normed, sigma = normed_rows(hidden, condition, gain)
    active = (normed * sigma).astype(jnp.bfloat16)
    weight = weight_ref[0]
    upper = hidden + jnp.dot(active, weight, preferred_element_type=jnp.float32)

    @pl.when(down)
    def _():
        out_ref[...] = sent_ref[...]
        active_ref[...] = first_active_ref[...]

    @pl.when(jnp.logical_not(down))
    def _():
        out_ref[...] = upper.astype(jnp.bfloat16)
        active_ref[...] = active

    target = rows_ref[0, number].astype(jnp.float32)
    cot = (upper - target) / math.sqrt(MICRO * ROWS * LANES)
    store_pieces(pieces_ref, 4, cot)
    cot = cot.astype(jnp.bfloat16)
    through = lax.dot_general(
        cot, weight, (((1,), (1,)), ((), ())), preferred_element_type=jnp.float32
    )
    scaled = through * sigma * (1.0 + normed * (1.0 - sigma)) * gain
    inner = jnp.mean(scaled * shifted, axis=-1, keepdims=True)
    back = cot.astype(jnp.float32) + inverse * scaled - shifted * inverse**3 * inner
    store_pieces(pieces_ref, 0, back)


def weight_kernel(*refs):
    active_refs, piece_refs, shares_ref = refs[:8], refs[8:10], refs[10]
    first, second, third, staged = refs[11:15]
    yl, core = lax.axis_index("yl"), lax.axis_index("core")
    low = lax.broadcasted_iota(jnp.int32, (ROWS // 2, 128), 1) < 64
    zero = jnp.zeros((ROWS // 2, 128), jnp.bfloat16)
    product = None
    for offset in range(4):
        source = ((yl + offset // 2) % 2) * 2 + (core + offset % 2) % 2
        rows, right = [], []
        for number in range(MICRO):
            rows.append(active_refs[number * 4 + offset][...])
            piece = piece_refs[number].at[4 + source]
            tail = piece[2 * ROWS :]
            right.append(
                jnp.concatenate(
                    [
                        piece[:ROWS],
                        piece[ROWS : 2 * ROWS],
                        jnp.concatenate([jnp.where(low, tail, zero), jnp.where(low, zero, tail)]),
                    ],
                    axis=1,
                )
            )
        term = lax.dot_general(
            jnp.concatenate(rows), jnp.concatenate(right), (((0,), (0,)), ((), ())),
            preferred_element_type=jnp.float32,
        )
        product = term if product is None else product + term
    first[...] = product[:, :128]
    second[...] = product[:, 128:256]
    third[...] = product[:, 256:] + pltpu.roll(product[:, 256:], 64, 1)
    few = lax.broadcasted_iota(jnp.int32, (5, 128), 1) < 64

    def pack(block, carry):
        base = pl.multiple_of(block * 80, 80)
        to = pl.multiple_of(block * 8 * SHARE, 8 * SHARE)
        for lane in range(8):
            at, put = base + 10 * lane, to + SHARE * lane
            staged[pl.ds(put, 10)] = first[pl.ds(at, 10)]
            staged[pl.ds(put + 16, 10)] = second[pl.ds(at, 10)]
            even = third[pl.ds(at, 5, 2)]
            odd = third[pl.ds(at + 1, 5, 2)]
            staged[pl.ds(put + 10, 5)] = jnp.where(few, even, odd)
        return carry

    staged[...] = jnp.zeros_like(staged)
    lax.fori_loop(0, LANES // 8, pack, 0)
    shares_ref[...] = staged[...].astype(jnp.bfloat16).reshape(LANES, SHARE, 128)


def total_kernel(shares_ref, gradient_ref, tail):
    low = lax.broadcasted_iota(jnp.int32, (5, 128), 1) < 64
    sums = []
    for quarter in range(4):
        yl, core = quarter // 2, quarter % 2
        acc = None
        for yh in range(2):
            for zx in range(16):
                lane = ((yh * 2 + yl) * 16 + zx) * 2 + core
                term = shares_ref[lane].astype(jnp.float32)
                acc = term if acc is None else acc + term
        gradient_ref[:, 256 * quarter : 256 * quarter + 128] = acc[:10]
        gradient_ref[:, 256 * quarter + 128 : 256 * quarter + 256] = acc[16:26]
        sums.append(acc[10:15])
    for pair in range(2):
        left, right = sums[2 * pair], sums[2 * pair + 1]
        at = 1024 + 128 * pair
        tail[pl.ds(0, 5, 2)] = jnp.where(low, left, pltpu.roll(right, 64, 1))
        tail[pl.ds(1, 5, 2)] = jnp.where(low, pltpu.roll(left, 64, 1), right)
        gradient_ref[:, at : at + 128] = tail[...]


def swap(block, axis):
    return lax.ppermute(block, axis, [(0, 1), (1, 0)])


def local(inputs, weights, gains, timesteps, text_pooled):
    half = jax.ShapeDtypeStruct((ROWS, C), jnp.bfloat16)
    sent, first_active, received = [], [], []
    for number in range(MICRO):
        out, active = pl.pallas_call(
            functools.partial(down_kernel, number),
            out_shape=(half, half),
            in_specs=[SMEM, VMEM, VMEM, VMEM, VMEM],
            out_specs=(VMEM, VMEM),
            compiler_params=PARAMS,
        )(timesteps, inputs, weights, gains, text_pooled)
        sent.append(out)
        first_active.append(active)
        received.append(lax.ppermute(out, "section", [(0, 1)]))
    outs, actives, arrived = [], [], []
    for number in range(MICRO):
        out, active, pieces = pl.pallas_call(
            functools.partial(up_kernel, number),
            out_shape=(half, half, jax.ShapeDtypeStruct((8, PIECE, 128), jnp.bfloat16)),
            in_specs=[SMEM] + [VMEM] * 7,
            out_specs=(VMEM, VMEM, VMEM),
            compiler_params=PARAMS,
        )(
            timesteps, received[number], inputs, weights, gains, text_pooled,
            sent[number], first_active[number],
        )
        outs.append(out)
        far = swap(active, "yl")
        near = swap(active, "core")
        actives += [active, near, far, swap(far, "core")]
        arrived.append(lax.all_to_all(pieces, ("section",) + GROUP, 0, 0, tiled=True))
    shares = pl.pallas_call(
        weight_kernel,
        out_shape=jax.ShapeDtypeStruct((LANES, SHARE, 128), jnp.bfloat16),
        in_specs=[VMEM] * 10,
        out_specs=VMEM,
        scratch_shapes=[
            pltpu.VMEM((C, 128), jnp.float32),
            pltpu.VMEM((C, 128), jnp.float32),
            pltpu.VMEM((C, 128), jnp.float32),
            pltpu.VMEM((LANES * SHARE, 128), jnp.float32),
        ],
        compiler_params=PARAMS,
    )(*actives, *arrived)
    shares = lax.all_to_all(shares, DP, 0, 0, tiled=True)
    gradient = pl.pallas_call(
        total_kernel,
        out_shape=jax.ShapeDtypeStruct((C // LANES, C), jnp.float32),
        in_specs=[VMEM],
        out_specs=VMEM,
        scratch_shapes=[pltpu.VMEM((C // LANES, 128), jnp.float32)],
        compiler_params=PARAMS,
    )(shares)
    return (jnp.stack(outs)[None], gradient[None])


def solution(mesh):
    fine = Mesh(mesh.devices.reshape(2, 2, 2, 8, 2, 2), ("section",) + DP)
    return jax.shard_map(
        local,
        mesh=fine,
        in_specs=(
            P("section", None, DP, None),
            P("section", None, None),
            P("section", None),
            P(),
            P(),
        ),
        out_specs=(P("section", None, DP, None), P("section", DP, None)),
        check_vma=False,
    )
```

```python
import functools
import math

import jax
import jax.numpy as jnp
from jax import lax
from jax.experimental import pallas as pl
from jax.experimental.pallas import tpu as pltpu
from jax.sharding import Mesh, PartitionSpec as P

PIX = 1024
MICRO = 2
ROWS = 128
LANES = 128
C = 1280
DP = ("yh", "yl", "z", "x", "core")
GROUP = ("yl", "core")
PIECE = 320
SHARE = 32
PARAMS = pltpu.CompilerParams(vmem_limit_bytes=40 * 1024 * 1024)
WHOLE = pltpu.CompilerParams(vmem_limit_bytes=61 * 1024 * 1024)
MOST = pltpu.CompilerParams(vmem_limit_bytes=53 * 1024 * 1024)
VMEM = pl.BlockSpec(memory_space=pltpu.VMEM)
HBM = pl.BlockSpec(memory_space=pltpu.HBM)


def condition_row(steps_ref, text_ref, number):
    latent = lax.axis_index(DP) * ROWS // PIX
    step = steps_ref[number, latent].astype(jnp.float32)
    lane = lax.broadcasted_iota(jnp.int32, (1, C), 1)
    index = jnp.where(lane < C // 2, lane, lane - C // 2).astype(jnp.float32)
    angle = step * jnp.exp(-math.log(10000.0) * index / (C // 2))
    waves = jnp.where(lane < C // 2, jnp.cos(angle), jnp.sin(angle))
    text = text_ref[number].astype(jnp.float32)
    mine = lax.broadcasted_iota(jnp.int32, text.shape, 0) == latent
    return waves + jnp.sum(jnp.where(mine, text, 0.0), axis=0, keepdims=True)


def normed_rows(hidden, condition, gain):
    shifted = hidden + condition
    inverse = lax.rsqrt(jnp.mean(shifted * shifted, axis=-1, keepdims=True) + 1e-05)
    normed = shifted * inverse * gain
    sigma = 1.0 / (1.0 + jnp.exp(-normed))
    return shifted, inverse, normed, sigma


def down_kernel(
    steps_hbm, rows_hbm, weight_hbm, gain_hbm, text_hbm, sent_0, sent_1, active_0, active_1, cond_ref,
    steps_ref, rows_ref, weight_ref, gain_ref, text_ref, sems,
):
    copies = [
        pltpu.make_async_copy(source, target, sems.at[at])
        for at, (source, target) in enumerate(
            (
                (steps_hbm, steps_ref),
                (text_hbm, text_ref),
                (rows_hbm.at[0], rows_ref),
                (gain_hbm, gain_ref),
                (weight_hbm.at[0], weight_ref),
            )
        )
    ]
    for copy in copies:
        copy.start()
    copies[0].wait()
    copies[1].wait()
    for number in range(MICRO):
        cond_ref[number] = condition_row(steps_ref, text_ref, number)
    copies[2].wait()
    copies[3].wait()
    for number, sent_ref, active_ref in ((0, sent_0, active_0), (1, sent_1, active_1)):
        hidden = rows_ref[number].astype(jnp.float32)
        _, _, normed, sigma = normed_rows(hidden, cond_ref[number], gain_ref[...])
        active = (normed * sigma).astype(jnp.bfloat16)
        active_ref[...] = active
        if number == 0:
            copies[4].wait()
        result = hidden + jnp.dot(active, weight_ref[...], preferred_element_type=jnp.float32)
        sent_ref[...] = result.astype(jnp.bfloat16)


def store_pieces(pieces_ref, first, values):
    half = ROWS // 2
    low = lax.broadcasted_iota(jnp.int32, (half, 128), 1) < 64
    rounded = values.astype(jnp.bfloat16)
    for quarter in range(4):
        slot = first + quarter
        pieces_ref[slot, :ROWS] = rounded[:, 256 * quarter : 256 * quarter + 128]
        pieces_ref[slot, ROWS : 2 * ROWS] = rounded[:, 256 * quarter + 128 : 256 * quarter + 256]
        at = 1024 + 128 * (quarter // 2)
        block = values[:, at : at + 128]
        turned = pltpu.roll(block, 64, 1)
        top, bottom = (block, turned) if quarter % 2 == 0 else (turned, block)
        pieces_ref[slot, 2 * ROWS :] = jnp.where(low, top[:half], bottom[half:]).astype(
            jnp.bfloat16
        )


def up_kernel(
    number, cond_ref, arrived_ref, rows_hbm, weight_hbm, gain_ref, sent_hbm, first_active_hbm,
    outs_in, outs_hbm, active_ref, pieces_hbm, out_ref, pieces_ref, rows_ref, sent_ref,
    first_active_ref, weight_ref, sems,
):
    del outs_in
    copies = [
        pltpu.make_async_copy(rows_hbm.at[0, number], rows_ref, sems.at[3]),
        pltpu.make_async_copy(sent_hbm, sent_ref, sems.at[4]),
        pltpu.make_async_copy(first_active_hbm, first_active_ref, sems.at[5]),
        pltpu.make_async_copy(weight_hbm.at[0], weight_ref, sems.at[6]),
    ]
    for copy in copies:
        copy.start()
    down = lax.axis_index("section") == 0
    gain = gain_ref[...]
    hidden = arrived_ref[...].astype(jnp.float32)
    shifted, inverse, normed, sigma = normed_rows(hidden, cond_ref[number], gain)
    active = (normed * sigma).astype(jnp.bfloat16)
    for copy in copies:
        copy.wait()
    weight = weight_ref[...]
    upper = hidden + jnp.dot(active, weight, preferred_element_type=jnp.float32)

    @pl.when(down)
    def _():
        out_ref[...] = sent_ref[...]
        active_ref[...] = first_active_ref[...]

    @pl.when(jnp.logical_not(down))
    def _():
        out_ref[...] = upper.astype(jnp.bfloat16)
        active_ref[...] = active

    out_copy = pltpu.make_async_copy(out_ref, outs_hbm.at[0, number], sems.at[0])
    out_copy.start()
    target = rows_ref[...].astype(jnp.float32)
    cot = (upper - target) / math.sqrt(MICRO * ROWS * LANES)
    store_pieces(pieces_ref, 4, cot)
    cot_copy = pltpu.make_async_copy(
        pieces_ref.at[pl.ds(4, 4)], pieces_hbm.at[pl.ds(4, 4)], sems.at[1]
    )
    cot_copy.start()
    cot = cot.astype(jnp.bfloat16)
    through = lax.dot_general(
        cot, weight, (((1,), (1,)), ((), ())), preferred_element_type=jnp.float32
    )
    scaled = through * sigma * (1.0 + normed * (1.0 - sigma)) * gain
    inner = jnp.mean(scaled * shifted, axis=-1, keepdims=True)
    back = cot.astype(jnp.float32) + inverse * scaled - shifted * inverse**3 * inner
    store_pieces(pieces_ref, 0, back)
    back_copy = pltpu.make_async_copy(
        pieces_ref.at[pl.ds(0, 4)], pieces_hbm.at[pl.ds(0, 4)], sems.at[2]
    )
    back_copy.start()
    out_copy.wait()
    cot_copy.wait()
    back_copy.wait()


def weight_product(active_refs, piece_ref):
    yl, core = lax.axis_index("yl"), lax.axis_index("core")
    low = lax.broadcasted_iota(jnp.int32, (ROWS // 2, 128), 1) < 64
    zero = jnp.zeros((ROWS // 2, 128), jnp.bfloat16)
    rows, right = [], []
    for offset in range(4):
        source = ((yl + offset // 2) % 2) * 2 + (core + offset % 2) % 2
        rows.append(active_refs[offset][...])
        piece = piece_ref.at[4 + source]
        tail = piece[2 * ROWS :]
        right.append(
            jnp.concatenate(
                [
                    piece[:ROWS],
                    piece[ROWS : 2 * ROWS],
                    jnp.concatenate([jnp.where(low, tail, zero), jnp.where(low, zero, tail)]),
                ],
                axis=1,
            )
        )
    return lax.dot_general(
        jnp.concatenate(rows), jnp.concatenate(right), (((0,), (0,)), ((), ())),
        preferred_element_type=jnp.float32,
    )


def first_weight_kernel(own, near, far, far_core, piece_ref, product_ref):
    product_ref[...] = weight_product((own, near, far, far_core), piece_ref)


def weight_kernel(
    own, near, far, far_core, piece_ref, earlier_ref, shares_ref, first, second, third, staged
):
    product = weight_product((own, near, far, far_core), piece_ref) + earlier_ref[...]
    first[...] = product[:, :128]
    second[...] = product[:, 128:256]
    third[...] = product[:, 256:] + pltpu.roll(product[:, 256:], 64, 1)
    few = lax.broadcasted_iota(jnp.int32, (5, 128), 1) < 64

    def pack(block, carry):
        base = pl.multiple_of(block * 80, 80)
        to = pl.multiple_of(block * 8 * SHARE, 8 * SHARE)
        for lane in range(8):
            at, put = base + 10 * lane, to + SHARE * lane
            staged[pl.ds(put, 10)] = first[pl.ds(at, 10)]
            staged[pl.ds(put + 16, 10)] = second[pl.ds(at, 10)]
            even = third[pl.ds(at, 5, 2)]
            odd = third[pl.ds(at + 1, 5, 2)]
            staged[pl.ds(put + 10, 5)] = jnp.where(few, even, odd)
        return carry

    staged[...] = jnp.zeros_like(staged)
    lax.fori_loop(0, LANES // 8, pack, 0)
    shares_ref[...] = staged[...].astype(jnp.bfloat16).reshape(LANES, SHARE, 128)


def total_kernel(shares_ref, gradient_ref, tail):
    low = lax.broadcasted_iota(jnp.int32, (5, 128), 1) < 64
    sums = []
    for quarter in range(4):
        yl, core = quarter // 2, quarter % 2
        acc = None
        for yh in range(2):
            for zx in range(16):
                lane = ((yh * 2 + yl) * 16 + zx) * 2 + core
                term = shares_ref[lane].astype(jnp.float32)
                acc = term if acc is None else acc + term
        gradient_ref[:, 0, 256 * quarter : 256 * quarter + 128] = acc[:10]
        gradient_ref[:, 0, 256 * quarter + 128 : 256 * quarter + 256] = acc[16:26]
        sums.append(acc[10:15])
    for pair in range(2):
        left, right = sums[2 * pair], sums[2 * pair + 1]
        at = 1024 + 128 * pair
        tail[pl.ds(0, 5, 2)] = jnp.where(low, left, pltpu.roll(right, 64, 1))
        tail[pl.ds(1, 5, 2)] = jnp.where(low, pltpu.roll(left, 64, 1), right)
        gradient_ref[:, 0, at : at + 128] = tail[...]


def swap(block, axis):
    return lax.ppermute(block, axis, [(0, 1), (1, 0)])


def local(inputs, weights, gains, timesteps, text_pooled):
    half = jax.ShapeDtypeStruct((ROWS, C), jnp.bfloat16)
    *made, condition = pl.pallas_call(
        down_kernel,
        out_shape=(half,) * 4 + (jax.ShapeDtypeStruct((MICRO, 1, C), jnp.float32),),
        in_specs=[HBM] * 5,
        out_specs=(VMEM,) * 5,
        scratch_shapes=[
            pltpu.SMEM(timesteps.shape, jnp.int32),
            pltpu.VMEM(inputs.shape[1:], jnp.bfloat16),
            pltpu.VMEM(weights.shape[1:], jnp.bfloat16),
            pltpu.VMEM(gains.shape, jnp.float32),
            pltpu.VMEM(text_pooled.shape, jnp.bfloat16),
            pltpu.SemaphoreType.DMA((5,)),
        ],
        compiler_params=WHOLE,
    )(timesteps, inputs, weights, gains, text_pooled)
    sent, first_active = made[:2], made[2:]
    received = [lax.ppermute(rows, "section", [(0, 1)]) for rows in sent]
    outs = None
    actives, arrived = [], []
    for number in range(MICRO):
        up = pl.pallas_call(
            functools.partial(up_kernel, number),
            out_shape=(
                jax.ShapeDtypeStruct(inputs.shape, jnp.bfloat16),
                half,
                jax.ShapeDtypeStruct((8, PIECE, 128), jnp.bfloat16),
            ),
            in_specs=[VMEM, VMEM, HBM, HBM, VMEM, HBM, HBM, HBM],
            out_specs=(HBM, VMEM, HBM),
            scratch_shapes=[
                pltpu.VMEM((ROWS, C), jnp.bfloat16),
                pltpu.VMEM((8, PIECE, 128), jnp.bfloat16),
                pltpu.VMEM((ROWS, C), jnp.bfloat16),
                pltpu.VMEM((ROWS, C), jnp.bfloat16),
                pltpu.VMEM((ROWS, C), jnp.bfloat16),
                pltpu.VMEM((C, C), jnp.bfloat16),
                pltpu.SemaphoreType.DMA((7,)),
            ],
            input_output_aliases={7: 0} if number else {},
            compiler_params=MOST,
            cost_estimate=pl.CostEstimate(flops=2_000_000_000, bytes_accessed=4_000_000, transcendentals=0),
        )
        outs, active, pieces = up(
            condition, received[number], inputs, weights, gains, sent[number],
            first_active[number], outs if number else inputs,
        )
        far = swap(active, "yl")
        near = swap(active, "core")
        actives.append((active, near, far, swap(far, "core")))
        arrived.append(lax.all_to_all(pieces, ("section",) + GROUP, 0, 0, tiled=True))
    earlier = pl.pallas_call(
        first_weight_kernel,
        out_shape=jax.ShapeDtypeStruct((C, 384), jnp.float32),
        in_specs=[VMEM] * 5,
        out_specs=VMEM,
        compiler_params=PARAMS,
        cost_estimate=pl.CostEstimate(flops=500_000_000, bytes_accessed=4_000_000, transcendentals=0),
    )(*actives[0], arrived[0])
    shares = pl.pallas_call(
        weight_kernel,
        out_shape=jax.ShapeDtypeStruct((LANES, SHARE, 128), jnp.bfloat16),
        in_specs=[VMEM] * 6,
        out_specs=VMEM,
        scratch_shapes=[
            pltpu.VMEM((C, 128), jnp.float32),
            pltpu.VMEM((C, 128), jnp.float32),
            pltpu.VMEM((C, 128), jnp.float32),
            pltpu.VMEM((LANES * SHARE, 128), jnp.float32),
        ],
        compiler_params=PARAMS,
    )(*actives[1], arrived[1], earlier)
    shares = lax.all_to_all(shares, DP, 0, 0, tiled=True)
    gradient = pl.pallas_call(
        total_kernel,
        out_shape=jax.ShapeDtypeStruct((C // LANES, 1, C), jnp.float32),
        in_specs=[VMEM],
        out_specs=VMEM,
        scratch_shapes=[pltpu.VMEM((C // LANES, 128), jnp.float32)],
        compiler_params=PARAMS,
    )(shares)
    return (outs, jnp.transpose(gradient, (1, 0, 2)))


def solution(mesh):
    fine = Mesh(mesh.devices.reshape(2, 2, 2, 8, 2, 2), ("section",) + DP)
    return jax.shard_map(
        local,
        mesh=fine,
        in_specs=(
            P("section", None, DP, None),
            P("section", None, None),
            P("section", None),
            P(),
            P(),
        ),
        out_specs=(P("section", None, DP, None), P("section", DP, None)),
        check_vma=False,
    )
```

```python
import functools
import math

import jax
import jax.numpy as jnp
from jax import lax
from jax.experimental import pallas as pl
from jax.experimental.pallas import tpu as pltpu
from jax.sharding import Mesh, PartitionSpec as P

PIX = 1024
MICRO = 2
ROWS = 128
LANES = 128
C = 1280
DP = ("y", "z", "x", "core")
PIECE = 320
SHARE = 16
TAIL = C + 8
PARAMS = pltpu.CompilerParams(vmem_limit_bytes=40 * 1024 * 1024)
WHOLE = pltpu.CompilerParams(vmem_limit_bytes=52 * 1024 * 1024)
MOST = pltpu.CompilerParams(vmem_limit_bytes=51 * 1024 * 1024)
VMEM = pl.BlockSpec(memory_space=pltpu.VMEM)
HBM = pl.BlockSpec(memory_space=pltpu.HBM)


def condition_row(steps_ref, text_ref, number):
    latent = lax.axis_index(DP) * ROWS // PIX
    step = steps_ref[number, latent].astype(jnp.float32)
    lane = lax.broadcasted_iota(jnp.int32, (1, C), 1)
    index = jnp.where(lane < C // 2, lane, lane - C // 2).astype(jnp.float32)
    angle = step * jnp.exp(-math.log(10000.0) * index / (C // 2))
    waves = jnp.where(lane < C // 2, jnp.cos(angle), jnp.sin(angle))
    text = text_ref[number].astype(jnp.float32)
    mine = lax.broadcasted_iota(jnp.int32, text.shape, 0) == latent
    return waves + jnp.sum(jnp.where(mine, text, 0.0), axis=0, keepdims=True)


def normed_rows(hidden, condition, gain):
    shifted = hidden + condition
    inverse = lax.rsqrt(jnp.mean(shifted * shifted, axis=-1, keepdims=True) + 1e-05)
    normed = shifted * inverse * gain
    sigma = 1.0 / (1.0 + jnp.exp(-normed))
    return shifted, inverse, normed, sigma


def down_kernel(
    steps_hbm, rows_hbm, weight_hbm, gain_hbm, text_hbm,
    sent_0, sent_1, active_0, active_1, cond_ref, weight_ref,
    steps_ref, rows_ref, gain_ref, text_ref, sems,
):
    copies = [
        pltpu.make_async_copy(source, target, sems.at[at])
        for at, (source, target) in enumerate(
            (
                (steps_hbm, steps_ref),
                (text_hbm, text_ref),
                (rows_hbm.at[0], rows_ref),
                (gain_hbm, gain_ref),
                (weight_hbm.at[0], weight_ref),
            )
        )
    ]
    for copy in copies:
        copy.start()
    copies[0].wait()
    copies[1].wait()
    for number in range(MICRO):
        cond_ref[number] = condition_row(steps_ref, text_ref, number)
    copies[2].wait()
    copies[3].wait()
    for number, sent_ref, active_ref in ((0, sent_0, active_0), (1, sent_1, active_1)):
        hidden = rows_ref[number].astype(jnp.float32)
        _, _, normed, sigma = normed_rows(hidden, cond_ref[number], gain_ref[...])
        active = (normed * sigma).astype(jnp.bfloat16)
        active_ref[...] = active
        if number == 0:
            copies[4].wait()
        result = hidden + jnp.dot(active, weight_ref[...], preferred_element_type=jnp.float32)
        sent_ref[...] = result.astype(jnp.bfloat16)


def store_pieces(pieces_ref, first, values):
    half = ROWS // 2
    low = lax.broadcasted_iota(jnp.int32, (half, 128), 1) < 64
    rounded = values.astype(jnp.bfloat16)
    y = lax.axis_index("y")
    for quarter in range(4):
        slot = first + lax.rem(quarter + 4 - y, 4)
        pieces_ref[slot, :ROWS] = rounded[:, 256 * quarter : 256 * quarter + 128]
        pieces_ref[slot, ROWS : 2 * ROWS] = rounded[:, 256 * quarter + 128 : 256 * quarter + 256]
        at = 1024 + 128 * (quarter // 2)
        block = values[:, at : at + 128]
        turned = pltpu.roll(block, 64, 1)
        top, bottom = (block, turned) if quarter % 2 == 0 else (turned, block)
        pieces_ref[slot, 2 * ROWS :] = jnp.where(low, top[:half], bottom[half:]).astype(
            jnp.bfloat16
        )


def up_kernel(number, *refs):
    cond_ref, arrived_ref, rows_hbm, weight_ref, gain_ref, sent_hbm, first_active_hbm = refs[:7]
    before = refs[7 : 7 + 9 * number]
    outs_hbm, active_hbm, *send_refs = refs[7 + 9 * number : 17 + 9 * number]
    out_ref, active_ref, pieces_ref, rows_ref, sems = refs[17 + 9 * number :]
    rows_copy = pltpu.make_async_copy(rows_hbm.at[0, number], rows_ref, sems.at[0])
    rows_copy.start()
    down = lax.axis_index("section") == 0
    kept = [
        pltpu.make_async_copy(sent_hbm, outs_hbm.at[0, number], sems.at[1]),
        pltpu.make_async_copy(first_active_hbm, active_hbm, sems.at[2]),
    ]
    made = [
        pltpu.make_async_copy(out_ref, outs_hbm.at[0, number], sems.at[1]),
        pltpu.make_async_copy(active_ref, active_hbm, sems.at[2]),
    ]

    @pl.when(down)
    def _():
        for copy in kept:
            copy.start()

    gain = gain_ref[...]
    hidden = arrived_ref[...].astype(jnp.float32)
    shifted, inverse, normed, sigma = normed_rows(hidden, cond_ref[number], gain)
    active = (normed * sigma).astype(jnp.bfloat16)
    active_ref[...] = active
    weight = weight_ref[...]
    upper = hidden + jnp.dot(active, weight, preferred_element_type=jnp.float32)
    out_ref[...] = upper.astype(jnp.bfloat16)

    @pl.when(jnp.logical_not(down))
    def _():
        for copy in made:
            copy.start()

    rows_copy.wait()
    cot = (upper - rows_ref[...].astype(jnp.float32)) / math.sqrt(MICRO * ROWS * LANES)
    store_pieces(pieces_ref, 4, cot)
    cot = cot.astype(jnp.bfloat16)
    through = lax.dot_general(
        cot, weight, (((1,), (1,)), ((), ())), preferred_element_type=jnp.float32
    )
    scaled = through * sigma * (1.0 + normed * (1.0 - sigma)) * gain
    inner = jnp.mean(scaled * shifted, axis=-1, keepdims=True)
    back = cot.astype(jnp.float32) + inverse * scaled - shifted * inverse**3 * inner
    store_pieces(pieces_ref, 0, back)
    for slot in range(8):
        if number:
            send_refs[slot][:PIECE] = before[1 + slot][...]
        send_refs[slot][PIECE * number :] = pieces_ref[slot]

    @pl.when(down)
    def _():
        for copy in kept:
            copy.wait()

    @pl.when(jnp.logical_not(down))
    def _():
        for copy in made:
            copy.wait()


def pack(main, tail, staged):
    group = lax.broadcasted_iota(jnp.int32, (3, 128), 1) // 32
    staged[...] = jnp.zeros_like(staged)

    def lanes(block, carry):
        base = pl.multiple_of(block * 80, 80)
        to = pl.multiple_of(block * 8 * SHARE, 8 * SHARE)
        for lane in range(8):
            at, put = base + 10 * lane, to + SHARE * lane
            staged[pl.ds(put, 10)] = main[pl.ds(at, 10)]
            row = tail[pl.ds(at, 3, 4)]
            for q in range(1, 4):
                row = jnp.where(group == q, tail[pl.ds(at + q, 3, 4)], row)
            staged[pl.ds(put + 10, 3)] = row
        return carry

    lax.fori_loop(0, LANES // 8, lanes, 0)


def weight_kernel(*refs):
    active_refs, back_refs, cot_refs = refs[:8], refs[8:12], refs[12:16]
    main_ref, tail_ref, away_ref, main, tail, staged = refs[16:]
    down, core = lax.axis_index("section") == 0, lax.axis_index("core")
    low = lax.broadcasted_iota(jnp.int32, (ROWS // 2, 128), 1) < 64
    zero = jnp.zeros((ROWS // 2, 128), jnp.bfloat16)
    product = None
    for offset in range(4):
        turn = (4 - offset) % 4
        rows, right = [], []
        for number in range(MICRO):
            rows.append(active_refs[number * 4 + offset][...])
            mine = pl.ds(PIECE * number, PIECE)
            piece = jnp.where(down, back_refs[turn][mine], cot_refs[turn][mine])
            end = piece[2 * ROWS :]
            right.append(
                jnp.concatenate(
                    [
                        piece[:ROWS],
                        piece[ROWS : 2 * ROWS],
                        jnp.concatenate([jnp.where(low, end, zero), jnp.where(low, zero, end)]),
                    ],
                    axis=1,
                )
            )
        term = lax.dot_general(
            jnp.concatenate(rows), jnp.concatenate(right), (((0,), (0,)), ((), ())),
            preferred_element_type=jnp.float32,
        )
        product = term if product is None else product + term
    first, second = product[:, :128], product[:, 128:256]
    both = product[:, 256:] + pltpu.roll(product[:, 256:], 64, 1)
    turned = pltpu.roll(both, 32, 1)
    even = (lax.broadcasted_iota(jnp.int32, both.shape, 1) // 32) % 2 == 0
    lower, upper = jnp.where(even, both, turned), jnp.where(even, turned, both)
    zeroth = core == 0
    main_ref[...] = jnp.where(zeroth, first, second)
    tail_ref[...] = jnp.where(zeroth, lower, upper)
    main[...] = jnp.where(zeroth, second, first)
    tail[:C] = jnp.where(zeroth, upper, lower)
    tail[C:] = jnp.zeros((TAIL - C, 128), jnp.float32)
    pack(main, tail, staged)
    away_ref[...] = staged[...].astype(jnp.bfloat16).reshape(LANES, SHARE, 128)


def pair_kernel(main_ref, tail_ref, other_ref, shares_ref, main, tail, staged):
    main[...] = main_ref[...]
    tail[:C] = tail_ref[...]
    tail[C:] = jnp.zeros((TAIL - C, 128), jnp.float32)
    pack(main, tail, staged)
    total = staged[...].reshape(LANES, SHARE, 128) + other_ref[...].astype(jnp.float32)
    shares_ref[...] = total.astype(jnp.bfloat16)


def total_kernel(shares_ref, gradient_ref, tail):
    group = lax.broadcasted_iota(jnp.int32, (3, 128), 1) // 32
    ends = []
    for y in range(4):
        for core in range(2):
            acc = None
            for zx in range(16):
                term = shares_ref[(y * 16 + zx) * 2 + core].astype(jnp.float32)
                acc = term if acc is None else acc + term
            at = 128 * (2 * y + core)
            gradient_ref[:, 0, at : at + 128] = acc[:10]
            ends.append(acc[10:13])
    for block in range(2):
        for q in range(4):
            row = None
            for g in range(4):
                end = ends[4 * block + g]
                end = end if g == q else pltpu.roll(end, (32 * (g - q)) % 128, 1)
                row = end if row is None else jnp.where(group == g, end, row)
            tail[pl.ds(q, 3, 4)] = row
        at = 1024 + 128 * block
        gradient_ref[:, 0, at : at + 128] = tail[:10]


def from_y(block, distance):
    return lax.ppermute(block, "y", [((i + distance) % 4, i) for i in range(4)])


def local(inputs, weights, gains, timesteps, text_pooled):
    half = jax.ShapeDtypeStruct((ROWS, C), jnp.bfloat16)
    whole = jax.ShapeDtypeStruct(inputs.shape, jnp.bfloat16)
    sent_0, sent_1, active_0, active_1, condition, weight = pl.pallas_call(
        down_kernel,
        out_shape=(half,) * 4
        + (
            jax.ShapeDtypeStruct((MICRO, 1, C), jnp.float32),
            jax.ShapeDtypeStruct((C, C), jnp.bfloat16),
        ),
        in_specs=[HBM] * 5,
        out_specs=(VMEM,) * 6,
        scratch_shapes=[
            pltpu.SMEM(timesteps.shape, jnp.int32),
            pltpu.VMEM(inputs.shape[1:], jnp.bfloat16),
            pltpu.VMEM(gains.shape, jnp.float32),
            pltpu.VMEM(text_pooled.shape, jnp.bfloat16),
            pltpu.SemaphoreType.DMA((5,)),
        ],
        compiler_params=WHOLE,
    )(timesteps, inputs, weights, gains, text_pooled)
    sent, first_active = (sent_0, sent_1), (active_0, active_1)
    received = [lax.ppermute(rows, "section", [(0, 1)]) for rows in sent]
    outs, pieces, actives = None, [], []
    for number in range(MICRO):
        piece = jax.ShapeDtypeStruct(((number + 1) * PIECE, 128), jnp.bfloat16)
        outs, active, *pieces = pl.pallas_call(
            functools.partial(up_kernel, number),
            out_shape=(whole, half) + (piece,) * 8,
            in_specs=[VMEM, VMEM, HBM, VMEM, VMEM, HBM, HBM] + ([HBM] + [VMEM] * 8) * number,
            out_specs=(HBM, HBM) + (VMEM,) * 8,
            scratch_shapes=[
                pltpu.VMEM((ROWS, C), jnp.bfloat16),
                pltpu.VMEM((ROWS, C), jnp.bfloat16),
                pltpu.VMEM((8, PIECE, 128), jnp.bfloat16),
                pltpu.VMEM((ROWS, C), jnp.bfloat16),
                pltpu.SemaphoreType.DMA((3,)),
            ],
            input_output_aliases={7: 0} if number else {},
            compiler_params=MOST,
            cost_estimate=pl.CostEstimate(
                flops=2_000_000_000, bytes_accessed=4_000_000, transcendentals=0
            ),
        )(
            condition, received[number], inputs, weight, gains, sent[number],
            first_active[number], *([outs, *pieces] if number else []),
        )
        ahead, behind = from_y(active, 1), from_y(active, -1)
        across = from_y(ahead, 1) if number == 0 else from_y(behind, -1)
        actives += [active, ahead, across, behind]
    returned = [
        lax.ppermute(pieces[r], ("section", "y"), [(4 + y, (y + r) % 4) for y in range(4)])
        for r in range(4)
    ]
    turned = [pieces[4]] + [
        lax.ppermute(pieces[4 + r], ("section", "y"), [(4 + y, 4 + (y + r) % 4) for y in range(4)])
        for r in range(1, 4)
    ]
    packed = [
        pltpu.VMEM((C, 128), jnp.float32),
        pltpu.VMEM((TAIL, 128), jnp.float32),
        pltpu.VMEM((LANES * SHARE, 128), jnp.float32),
    ]
    share = jax.ShapeDtypeStruct((LANES, SHARE, 128), jnp.bfloat16)
    main, tail, away = pl.pallas_call(
        weight_kernel,
        out_shape=(jax.ShapeDtypeStruct((C, 128), jnp.float32),) * 2 + (share,),
        in_specs=[VMEM] * 16,
        out_specs=(VMEM,) * 3,
        scratch_shapes=packed,
        compiler_params=PARAMS,
    )(*actives, *returned, *turned)
    other = lax.ppermute(away, "core", [(0, 1), (1, 0)])
    shares = pl.pallas_call(
        pair_kernel,
        out_shape=share,
        in_specs=[VMEM] * 3,
        out_specs=VMEM,
        scratch_shapes=packed,
        compiler_params=PARAMS,
    )(main, tail, other)
    shares = lax.all_to_all(shares, DP, 0, 0, tiled=True)
    gradient = pl.pallas_call(
        total_kernel,
        out_shape=jax.ShapeDtypeStruct((C // LANES, 1, C), jnp.float32),
        in_specs=[VMEM],
        out_specs=VMEM,
        scratch_shapes=[pltpu.VMEM((12, 128), jnp.float32)],
        compiler_params=PARAMS,
    )(shares)
    return (outs, jnp.transpose(gradient, (1, 0, 2)))


def solution(mesh):
    fine = Mesh(mesh.devices.reshape(2, 4, 8, 2, 2), ("section",) + DP)
    return jax.shard_map(
        local,
        mesh=fine,
        in_specs=(
            P("section", None, DP, None),
            P("section", None, None),
            P("section", None),
            P(),
            P(),
        ),
        out_specs=(P("section", None, DP, None), P("section", DP, None)),
        check_vma=False,
    )
```

```python
import functools
import math

import jax
import jax.numpy as jnp
from jax import lax
from jax.experimental import pallas as pl
from jax.experimental.pallas import tpu as pltpu
from jax.sharding import Mesh, PartitionSpec as P

PIX = 1024
MICRO = 2
ROWS = 128
LANES = 128
C = 1280
DP = ("y", "z", "x", "core")
COST = 50_000_000_000
PIECE = 320
SHARE = 16
TAIL = C + 8
PARAMS = pltpu.CompilerParams(vmem_limit_bytes=40 * 1024 * 1024)
WHOLE = pltpu.CompilerParams(vmem_limit_bytes=52 * 1024 * 1024)
MOST = pltpu.CompilerParams(vmem_limit_bytes=51 * 1024 * 1024)
VMEM = pl.BlockSpec(memory_space=pltpu.VMEM)
HBM = pl.BlockSpec(memory_space=pltpu.HBM)


def condition_row(steps_ref, text_ref, number):
    latent = lax.axis_index(DP) * ROWS // PIX
    step = steps_ref[number, latent].astype(jnp.float32)
    lane = lax.broadcasted_iota(jnp.int32, (1, C), 1)
    index = jnp.where(lane < C // 2, lane, lane - C // 2).astype(jnp.float32)
    angle = step * jnp.exp(-math.log(10000.0) * index / (C // 2))
    waves = jnp.where(lane < C // 2, jnp.cos(angle), jnp.sin(angle))
    text = text_ref[number].astype(jnp.float32)
    mine = lax.broadcasted_iota(jnp.int32, text.shape, 0) == latent
    return waves + jnp.sum(jnp.where(mine, text, 0.0), axis=0, keepdims=True)


def normed_rows(hidden, condition, gain):
    shifted = hidden + condition
    inverse = lax.rsqrt(jnp.mean(shifted * shifted, axis=-1, keepdims=True) + 1e-05)
    normed = shifted * inverse * gain
    sigma = 1.0 / (1.0 + jnp.exp(-normed))
    return shifted, inverse, normed, sigma


def down_kernel(
    steps_hbm, rows_hbm, weight_hbm, gain_hbm, text_hbm,
    sent_0, sent_1, active_0, active_1, cond_ref, weight_ref,
    steps_ref, rows_ref, gain_ref, text_ref, sems,
):
    copies = [
        pltpu.make_async_copy(source, target, sems.at[at])
        for at, (source, target) in enumerate(
            (
                (steps_hbm, steps_ref),
                (text_hbm, text_ref),
                (rows_hbm.at[0], rows_ref),
                (gain_hbm, gain_ref),
                (weight_hbm.at[0], weight_ref),
            )
        )
    ]
    for copy in copies:
        copy.start()
    copies[0].wait()
    copies[1].wait()
    for number in range(MICRO):
        cond_ref[number] = condition_row(steps_ref, text_ref, number)
    copies[2].wait()
    copies[3].wait()
    for number, sent_ref, active_ref in ((0, sent_0, active_0), (1, sent_1, active_1)):
        hidden = rows_ref[number].astype(jnp.float32)
        _, _, normed, sigma = normed_rows(hidden, cond_ref[number], gain_ref[...])
        active = (normed * sigma).astype(jnp.bfloat16)
        active_ref[...] = active
        if number == 0:
            copies[4].wait()
        result = hidden + jnp.dot(active, weight_ref[...], preferred_element_type=jnp.float32)
        sent_ref[...] = result.astype(jnp.bfloat16)


def store_pieces(pieces_ref, first, values):
    half = ROWS // 2
    low = lax.broadcasted_iota(jnp.int32, (half, 128), 1) < 64
    rounded = values.astype(jnp.bfloat16)
    for quarter in range(4):
        slot = first + quarter
        pieces_ref[slot, :ROWS] = rounded[:, 256 * quarter : 256 * quarter + 128]
        pieces_ref[slot, ROWS : 2 * ROWS] = rounded[:, 256 * quarter + 128 : 256 * quarter + 256]
        at = 1024 + 128 * (quarter // 2)
        block = values[:, at : at + 128]
        turned = pltpu.roll(block, 64, 1)
        top, bottom = (block, turned) if quarter % 2 == 0 else (turned, block)
        pieces_ref[slot, 2 * ROWS :] = jnp.where(low, top[:half], bottom[half:]).astype(
            jnp.bfloat16
        )


def up_kernel(number, *refs):
    cond_ref, arrived_ref, rows_hbm, weight_ref, gain_ref, sent_hbm, first_active_hbm = refs[:7]
    outs_hbm, actives_hbm, pieces_hbm = refs[7 + 3 * number : 10 + 3 * number]
    out_ref, active_ref, pieces_ref, rows_ref, sems = refs[10 + 3 * number :]
    active_hbm = actives_hbm.at[pl.ds(ROWS * number, ROWS)]
    rows_copy = pltpu.make_async_copy(rows_hbm.at[0, number], rows_ref, sems.at[0])
    rows_copy.start()
    down = lax.axis_index("section") == 0
    kept = [
        pltpu.make_async_copy(sent_hbm, outs_hbm.at[0, number], sems.at[1]),
        pltpu.make_async_copy(first_active_hbm, active_hbm, sems.at[2]),
    ]
    made = [
        pltpu.make_async_copy(out_ref, outs_hbm.at[0, number], sems.at[1]),
        pltpu.make_async_copy(active_ref, active_hbm, sems.at[2]),
    ]

    @pl.when(down)
    def _():
        for copy in kept:
            copy.start()

    gain = gain_ref[...]
    hidden = arrived_ref[...].astype(jnp.float32)
    shifted, inverse, normed, sigma = normed_rows(hidden, cond_ref[number], gain)
    active = (normed * sigma).astype(jnp.bfloat16)
    active_ref[...] = active
    weight = weight_ref[...]
    upper = hidden + jnp.dot(active, weight, preferred_element_type=jnp.float32)
    out_ref[...] = upper.astype(jnp.bfloat16)

    @pl.when(jnp.logical_not(down))
    def _():
        for copy in made:
            copy.start()

    rows_copy.wait()
    cot = (upper - rows_ref[...].astype(jnp.float32)) / math.sqrt(MICRO * ROWS * LANES)
    store_pieces(pieces_ref, 4, cot)
    mine = pl.ds(PIECE * number, PIECE)
    sends = [
        pltpu.make_async_copy(
            pieces_ref.at[pl.ds(at, 4)], pieces_hbm.at[pl.ds(at, 4), mine], sems.at[sem]
        )
        for at, sem in ((4, 3), (0, 4))
    ]
    sends[0].start()
    cot = cot.astype(jnp.bfloat16)
    through = lax.dot_general(
        cot, weight, (((1,), (1,)), ((), ())), preferred_element_type=jnp.float32
    )
    scaled = through * sigma * (1.0 + normed * (1.0 - sigma)) * gain
    inner = jnp.mean(scaled * shifted, axis=-1, keepdims=True)
    back = cot.astype(jnp.float32) + inverse * scaled - shifted * inverse**3 * inner
    store_pieces(pieces_ref, 0, back)
    sends[1].start()
    for send in sends:
        send.wait()

    @pl.when(down)
    def _():
        for copy in kept:
            copy.wait()

    @pl.when(jnp.logical_not(down))
    def _():
        for copy in made:
            copy.wait()


def pack(main, tail, staged):
    group = lax.broadcasted_iota(jnp.int32, (3, 128), 1) // 32
    staged[...] = jnp.zeros_like(staged)

    def lanes(block, carry):
        base = pl.multiple_of(block * 80, 80)
        to = pl.multiple_of(block * 8 * SHARE, 8 * SHARE)
        for lane in range(8):
            at, put = base + 10 * lane, to + SHARE * lane
            staged[pl.ds(put, 10)] = main[pl.ds(at, 10)]
            row = tail[pl.ds(at, 3, 4)]
            for q in range(1, 4):
                row = jnp.where(group == q, tail[pl.ds(at + q, 3, 4)], row)
            staged[pl.ds(put + 10, 3)] = row
        return carry

    lax.fori_loop(0, LANES // 8, lanes, 0)


def gathered_kernel(*refs):
    refs[-1][...] = jnp.zeros_like(refs[-1])


def weight_kernel(*refs):
    active_refs, piece_ref = refs[:4], refs[4]
    main_ref, tail_ref, away_ref, main, tail, staged = refs[6:]
    core = lax.axis_index("core")
    own = 2 * lax.rem(lax.axis_index("y"), 2) + lax.rem(lax.axis_index("z"), 2)
    low = lax.broadcasted_iota(jnp.int32, (ROWS // 2, 128), 1) < 64
    zero = jnp.zeros((ROWS // 2, 128), jnp.bfloat16)
    product = None
    for turn in range(4):
        right = []
        for number in range(MICRO):
            mine = pl.ds(PIECE * number, PIECE)
            piece = piece_ref[4 + lax.bitwise_xor(own, turn), mine]
            end = piece[2 * ROWS :]
            right.append(
                jnp.concatenate(
                    [
                        piece[:ROWS],
                        piece[ROWS : 2 * ROWS],
                        jnp.concatenate([jnp.where(low, end, zero), jnp.where(low, zero, end)]),
                    ],
                    axis=1,
                )
            )
        term = lax.dot_general(
            active_refs[turn][...], jnp.concatenate(right), (((0,), (0,)), ((), ())),
            preferred_element_type=jnp.float32,
        )
        product = term if product is None else product + term
    first, second = product[:, :128], product[:, 128:256]
    both = product[:, 256:] + pltpu.roll(product[:, 256:], 64, 1)
    turned = pltpu.roll(both, 32, 1)
    even = (lax.broadcasted_iota(jnp.int32, both.shape, 1) // 32) % 2 == 0
    lower, upper = jnp.where(even, both, turned), jnp.where(even, turned, both)
    zeroth = core == 0
    main_ref[...] = jnp.where(zeroth, first, second)
    tail_ref[...] = jnp.where(zeroth, lower, upper)
    main[...] = jnp.where(zeroth, second, first)
    tail[:C] = jnp.where(zeroth, upper, lower)
    tail[C:] = jnp.zeros((TAIL - C, 128), jnp.float32)
    pack(main, tail, staged)
    away_ref[...] = staged[...].astype(jnp.bfloat16).reshape(LANES, SHARE, 128)


def pair_kernel(main_ref, tail_ref, other_ref, shares_ref, main, tail, staged):
    main[...] = main_ref[...]
    tail[:C] = tail_ref[...]
    tail[C:] = jnp.zeros((TAIL - C, 128), jnp.float32)
    pack(main, tail, staged)
    total = staged[...].reshape(LANES, SHARE, 128) + other_ref[...].astype(jnp.float32)
    shares_ref[...] = total.astype(jnp.bfloat16)


def total_kernel(shares_ref, gradient_ref, tail):
    group = lax.broadcasted_iota(jnp.int32, (3, 128), 1) // 32
    ends = []
    for quarter in range(4):
        for core in range(2):
            acc = None
            for k in range(16):
                y, z, x = quarter // 2 + 2 * (k // 8), quarter % 2 + 2 * (k // 2 % 4), k % 2
                lane = ((y * 8 + z) * 2 + x) * 2 + core
                term = shares_ref[lane].astype(jnp.float32)
                acc = term if acc is None else acc + term
            at = 128 * (2 * quarter + core)
            gradient_ref[:, 0, at : at + 128] = acc[:10]
            ends.append(acc[10:13])
    for block in range(2):
        for q in range(4):
            row = None
            for g in range(4):
                end = ends[4 * block + g]
                end = end if g == q else pltpu.roll(end, (32 * (g - q)) % 128, 1)
                row = end if row is None else jnp.where(group == g, end, row)
            tail[pl.ds(q, 3, 4)] = row
        at = 1024 + 128 * block
        gradient_ref[:, 0, at : at + 128] = tail[:10]


def partner(y, z, core, t):
    y = ((y + core) % 4 ^ 1) - core if t & 2 else y
    z = ((z + core) % 8 ^ 1) - core if t & 1 else z
    return ((y % 4) * 8 + z % 8) * 2 + core


def squares():
    groups = []
    for x in range(2):
        for core in range(2):
            for y in range(0, 4, 2):
                for z in range(0, 8, 2):
                    group = []
                    for section in range(2):
                        for quarter in range(4):
                            near = (y + core + (quarter // 2 + core) % 2) % 4
                            side = (z + core + (quarter % 2 + core) % 2) % 8
                            group.append((((section * 4 + near) * 8 + side) * 2 + x) * 2 + core)
                    groups.append(group)
    return groups


def exchange(block, t, moves):
    at = [(y, z, core) for y in range(4) for z in range(8) for core in range(2)]
    route = [
        (64 * source + partner(*place, 0), 64 * target + partner(*place, t))
        for source, target in moves
        for place in at
    ]
    return lax.ppermute(block, ("section", "y", "z", "core"), route)


def local(inputs, weights, gains, timesteps, text_pooled):
    half = jax.ShapeDtypeStruct((ROWS, C), jnp.bfloat16)
    whole = jax.ShapeDtypeStruct(inputs.shape, jnp.bfloat16)
    sent_0, sent_1, active_0, active_1, condition, weight = pl.pallas_call(
        down_kernel,
        out_shape=(half,) * 4
        + (
            jax.ShapeDtypeStruct((MICRO, 1, C), jnp.float32),
            jax.ShapeDtypeStruct((C, C), jnp.bfloat16),
        ),
        in_specs=[HBM] * 5,
        out_specs=(VMEM,) * 6,
        scratch_shapes=[
            pltpu.SMEM(timesteps.shape, jnp.int32),
            pltpu.VMEM(inputs.shape[1:], jnp.bfloat16),
            pltpu.VMEM(gains.shape, jnp.float32),
            pltpu.VMEM(text_pooled.shape, jnp.bfloat16),
            pltpu.SemaphoreType.DMA((5,)),
        ],
        compiler_params=WHOLE,
    )(timesteps, inputs, weights, gains, text_pooled)
    sent, first_active = (sent_0, sent_1), (active_0, active_1)
    received = [lax.ppermute(rows, "section", [(0, 1)]) for rows in sent]
    outs, actives, pieces = None, None, None
    slots = jax.ShapeDtypeStruct((8, MICRO * PIECE, 128), jnp.bfloat16)
    both = jax.ShapeDtypeStruct((MICRO * ROWS, C), jnp.bfloat16)
    for number in range(MICRO):
        outs, actives, pieces = pl.pallas_call(
            functools.partial(up_kernel, number),
            out_shape=(whole, both, slots),
            in_specs=[VMEM, VMEM, HBM, VMEM, VMEM, HBM, HBM] + [HBM] * (3 * number),
            out_specs=(HBM,) * 3,
            scratch_shapes=[
                pltpu.VMEM((ROWS, C), jnp.bfloat16),
                pltpu.VMEM((ROWS, C), jnp.bfloat16),
                pltpu.VMEM((8, PIECE, 128), jnp.bfloat16),
                pltpu.VMEM((ROWS, C), jnp.bfloat16),
                pltpu.SemaphoreType.DMA((5,)),
            ],
            input_output_aliases={7: 0, 8: 1, 9: 2} if number else {},
            compiler_params=MOST,
            cost_estimate=pl.CostEstimate(
                flops=2_000_000_000, bytes_accessed=4_000_000, transcendentals=0
            ),
        )(
            condition, received[number], inputs, weight, gains, sent[number],
            first_active[number], *([outs, actives, pieces] if number else []),
        )
    others = [exchange(actives, t, ((0, 0), (1, 1))) for t in range(1, 4)]
    arrived = lax.all_to_all(
        pieces, ("section",) + DP, 0, 0, axis_index_groups=squares(), tiled=True
    )
    packed = [
        pltpu.VMEM((C, 128), jnp.float32),
        pltpu.VMEM((TAIL, 128), jnp.float32),
        pltpu.VMEM((LANES * SHARE, 128), jnp.float32),
    ]
    share = jax.ShapeDtypeStruct((LANES, SHARE, 128), jnp.bfloat16)
    gathered = pl.pallas_call(
        gathered_kernel,
        out_shape=jax.ShapeDtypeStruct((8, 128), jnp.float32),
        in_specs=[HBM] * 3,
        out_specs=VMEM,
        compiler_params=PARAMS,
        cost_estimate=pl.CostEstimate(flops=COST, bytes_accessed=2_000_000, transcendentals=0),
    )(*others)
    main, tail, away = pl.pallas_call(
        weight_kernel,
        out_shape=(jax.ShapeDtypeStruct((C, 128), jnp.float32),) * 2 + (share,),
        in_specs=[VMEM] * 5 + [HBM],
        out_specs=(VMEM,) * 3,
        scratch_shapes=packed,
        compiler_params=PARAMS,
    )(actives, *others, arrived, gathered)
    other = lax.ppermute(away, "core", [(0, 1), (1, 0)])
    shares = pl.pallas_call(
        pair_kernel,
        out_shape=share,
        in_specs=[VMEM] * 3,
        out_specs=VMEM,
        scratch_shapes=packed,
        compiler_params=PARAMS,
    )(main, tail, other)
    shares = lax.all_to_all(shares, DP, 0, 0, tiled=True)
    gradient = pl.pallas_call(
        total_kernel,
        out_shape=jax.ShapeDtypeStruct((C // LANES, 1, C), jnp.float32),
        in_specs=[VMEM],
        out_specs=VMEM,
        scratch_shapes=[pltpu.VMEM((12, 128), jnp.float32)],
        compiler_params=PARAMS,
    )(shares)
    return (outs, jnp.transpose(gradient, (1, 0, 2)))


def solution(mesh):
    fine = Mesh(mesh.devices.reshape(2, 4, 8, 2, 2), ("section",) + DP)
    return jax.shard_map(
        local,
        mesh=fine,
        in_specs=(
            P("section", None, DP, None),
            P("section", None, None),
            P("section", None),
            P(),
            P(),
        ),
        out_specs=(P("section", None, DP, None), P("section", DP, None)),
        check_vma=False,
    )
```

```python
import functools
import math

import jax
import jax.numpy as jnp
from jax import lax
from jax.experimental import pallas as pl
from jax.experimental.pallas import tpu as pltpu
from jax.sharding import Mesh, PartitionSpec as P

PIX = 1024
MICRO = 2
ROWS = 128
LANES = 128
C = 1280
DP = ("y", "z", "x", "core")
COST = 50_000_000_000
PIECE = 320
SHARE = 16
TAIL = C + 8
PARAMS = pltpu.CompilerParams(vmem_limit_bytes=40 * 1024 * 1024)
WHOLE = pltpu.CompilerParams(vmem_limit_bytes=52 * 1024 * 1024)
MOST = pltpu.CompilerParams(vmem_limit_bytes=51 * 1024 * 1024)
VMEM = pl.BlockSpec(memory_space=pltpu.VMEM)
HBM = pl.BlockSpec(memory_space=pltpu.HBM)


def condition_row(steps_ref, text_ref, number):
    latent = lax.axis_index(DP) * ROWS // PIX
    step = steps_ref[number, latent].astype(jnp.float32)
    lane = lax.broadcasted_iota(jnp.int32, (1, C), 1)
    index = jnp.where(lane < C // 2, lane, lane - C // 2).astype(jnp.float32)
    angle = step * jnp.exp(-math.log(10000.0) * index / (C // 2))
    waves = jnp.where(lane < C // 2, jnp.cos(angle), jnp.sin(angle))
    text = text_ref[number].astype(jnp.float32)
    mine = lax.broadcasted_iota(jnp.int32, text.shape, 0) == latent
    return waves + jnp.sum(jnp.where(mine, text, 0.0), axis=0, keepdims=True)


def normed_rows(hidden, condition, gain):
    shifted = hidden + condition
    inverse = lax.rsqrt(jnp.mean(shifted * shifted, axis=-1, keepdims=True) + 1e-05)
    normed = shifted * inverse * gain
    sigma = 1.0 / (1.0 + jnp.exp(-normed))
    return shifted, inverse, normed, sigma


def down_kernel(
    steps_hbm, rows_hbm, weight_hbm, gain_hbm, text_hbm,
    sent_0, sent_1, active_0, active_1, cond_ref, weight_ref,
    steps_ref, rows_ref, gain_ref, text_ref, sems,
):
    copies = [
        pltpu.make_async_copy(source, target, sems.at[at])
        for at, (source, target) in enumerate(
            (
                (steps_hbm, steps_ref),
                (text_hbm, text_ref),
                (rows_hbm.at[0], rows_ref),
                (gain_hbm, gain_ref),
                (weight_hbm.at[0], weight_ref),
            )
        )
    ]
    for copy in copies:
        copy.start()
    copies[0].wait()
    copies[1].wait()
    for number in range(MICRO):
        cond_ref[number] = condition_row(steps_ref, text_ref, number)
    copies[2].wait()
    copies[3].wait()
    for number, sent_ref, active_ref in ((0, sent_0, active_0), (1, sent_1, active_1)):
        hidden = rows_ref[number].astype(jnp.float32)
        _, _, normed, sigma = normed_rows(hidden, cond_ref[number], gain_ref[...])
        active = (normed * sigma).astype(jnp.bfloat16)
        active_ref[...] = active
        if number == 0:
            copies[4].wait()
        result = hidden + jnp.dot(active, weight_ref[...], preferred_element_type=jnp.float32)
        sent_ref[...] = result.astype(jnp.bfloat16)


def own_quarter():
    return 2 * lax.rem(lax.axis_index("y"), 2) + lax.rem(lax.axis_index("z"), 2)


def store_pieces(pieces_ref, first, values):
    half = ROWS // 2
    low = lax.broadcasted_iota(jnp.int32, (half, 128), 1) < 64
    rounded = values.astype(jnp.bfloat16)
    for quarter in range(4):
        slot = first + quarter
        pieces_ref[slot, :ROWS] = rounded[:, 256 * quarter : 256 * quarter + 128]
        pieces_ref[slot, ROWS : 2 * ROWS] = rounded[:, 256 * quarter + 128 : 256 * quarter + 256]
        at = 1024 + 128 * (quarter // 2)
        block = values[:, at : at + 128]
        turned = pltpu.roll(block, 64, 1)
        top, bottom = (block, turned) if quarter % 2 == 0 else (turned, block)
        pieces_ref[slot, 2 * ROWS :] = jnp.where(low, top[:half], bottom[half:]).astype(
            jnp.bfloat16
        )


def up_kernel(number, *refs):
    cond_ref, arrived_ref, rows_hbm, weight_ref, gain_ref, sent_hbm, first_active_hbm = refs[:7]
    outs_hbm, actives_hbm, *send_refs = refs[7 + 2 * number : -5]
    out_ref, active_ref, pieces_ref, rows_ref, sems = refs[-5:]
    active_hbm = actives_hbm.at[pl.ds(ROWS * number, ROWS)]
    rows_copy = pltpu.make_async_copy(rows_hbm.at[0, number], rows_ref, sems.at[0])
    rows_copy.start()
    down = lax.axis_index("section") == 0
    kept = [
        pltpu.make_async_copy(sent_hbm, outs_hbm.at[0, number], sems.at[1]),
        pltpu.make_async_copy(first_active_hbm, active_hbm, sems.at[2]),
    ]
    made = [
        pltpu.make_async_copy(out_ref, outs_hbm.at[0, number], sems.at[1]),
        pltpu.make_async_copy(active_ref, active_hbm, sems.at[2]),
    ]

    @pl.when(down)
    def _():
        for copy in kept:
            copy.start()

    gain = gain_ref[...]
    hidden = arrived_ref[...].astype(jnp.float32)
    shifted, inverse, normed, sigma = normed_rows(hidden, cond_ref[number], gain)
    active = (normed * sigma).astype(jnp.bfloat16)
    active_ref[...] = active
    weight = weight_ref[...]
    upper = hidden + jnp.dot(active, weight, preferred_element_type=jnp.float32)
    out_ref[...] = upper.astype(jnp.bfloat16)

    @pl.when(jnp.logical_not(down))
    def _():
        for copy in made:
            copy.start()

    rows_copy.wait()
    cot = (upper - rows_ref[...].astype(jnp.float32)) / math.sqrt(MICRO * ROWS * LANES)
    if number:
        store_pieces(pieces_ref, 4, cot)
        sends = [
            pltpu.make_async_copy(
                pieces_ref.at[pl.ds(at, 4)], send_refs[0].at[pl.ds(at, 4)], sems.at[sem]
            )
            for at, sem in ((4, 3), (0, 4))
        ]
        sends[0].start()
    else:
        store_pieces(pieces_ref, 4, cot)
        own = own_quarter()
        for turn in range(4):
            send_refs[turn][...] = pieces_ref[4 + lax.bitwise_xor(own, turn)]
    cot = cot.astype(jnp.bfloat16)
    through = lax.dot_general(
        cot, weight, (((1,), (1,)), ((), ())), preferred_element_type=jnp.float32
    )
    scaled = through * sigma * (1.0 + normed * (1.0 - sigma)) * gain
    inner = jnp.mean(scaled * shifted, axis=-1, keepdims=True)
    back = cot.astype(jnp.float32) + inverse * scaled - shifted * inverse**3 * inner
    if number:
        store_pieces(pieces_ref, 0, back)
        sends[1].start()
        for send in sends:
            send.wait()
    else:
        send_refs[4][...] = back.astype(jnp.bfloat16)

    @pl.when(down)
    def _():
        for copy in kept:
            copy.wait()

    @pl.when(jnp.logical_not(down))
    def _():
        for copy in made:
            copy.wait()


def pack(main, tail, staged):
    group = lax.broadcasted_iota(jnp.int32, (3, 128), 1) // 32
    staged[...] = jnp.zeros_like(staged)

    def lanes(block, carry):
        base = pl.multiple_of(block * 80, 80)
        to = pl.multiple_of(block * 8 * SHARE, 8 * SHARE)
        for lane in range(8):
            at, put = base + 10 * lane, to + SHARE * lane
            staged[pl.ds(put, 10)] = main[pl.ds(at, 10)]
            row = tail[pl.ds(at, 3, 4)]
            for q in range(1, 4):
                row = jnp.where(group == q, tail[pl.ds(at + q, 3, 4)], row)
            staged[pl.ds(put + 10, 3)] = row
        return carry

    lax.fori_loop(0, LANES // 8, lanes, 0)


def returned_kernel(rows_ref, pieces_in, pieces_hbm, pieces_ref, sem):
    del pieces_in

    @pl.when(lax.axis_index("section") == 0)
    def _():
        store_pieces(pieces_ref, 0, rows_ref[...].astype(jnp.float32))
        copy = pltpu.make_async_copy(pieces_ref, pieces_hbm.at[pl.ds(0, 4)], sem)
        copy.start()
        copy.wait()


def gathered_kernel(*refs):
    refs[-1][...] = jnp.zeros_like(refs[-1])


def weight_kernel(*refs):
    active_refs, piece_ref, cot_refs = refs[:4], refs[4], refs[5:9]
    main_ref, tail_ref, away_ref, main, tail, staged = refs[10:]
    down, core = lax.axis_index("section") == 0, lax.axis_index("core")
    own = own_quarter()
    low = lax.broadcasted_iota(jnp.int32, (ROWS // 2, 128), 1) < 64
    zero = jnp.zeros((ROWS // 2, 128), jnp.bfloat16)
    product = None
    for turn in range(4):
        right = []
        for number in range(MICRO):
            piece = piece_ref[4 * number + lax.bitwise_xor(own, turn)]
            if number == 0:
                piece = jnp.where(down, piece, cot_refs[turn][...])
            end = piece[2 * ROWS :]
            right.append(
                jnp.concatenate(
                    [
                        piece[:ROWS],
                        piece[ROWS : 2 * ROWS],
                        jnp.concatenate([jnp.where(low, end, zero), jnp.where(low, zero, end)]),
                    ],
                    axis=1,
                )
            )
        term = lax.dot_general(
            active_refs[turn][...], jnp.concatenate(right), (((0,), (0,)), ((), ())),
            preferred_element_type=jnp.float32,
        )
        product = term if product is None else product + term
    first, second = product[:, :128], product[:, 128:256]
    both = product[:, 256:] + pltpu.roll(product[:, 256:], 64, 1)
    turned = pltpu.roll(both, 32, 1)
    even = (lax.broadcasted_iota(jnp.int32, both.shape, 1) // 32) % 2 == 0
    lower, upper = jnp.where(even, both, turned), jnp.where(even, turned, both)
    zeroth = core == 0
    main_ref[...] = jnp.where(zeroth, first, second)
    tail_ref[...] = jnp.where(zeroth, lower, upper)
    main[...] = jnp.where(zeroth, second, first)
    tail[:C] = jnp.where(zeroth, upper, lower)
    tail[C:] = jnp.zeros((TAIL - C, 128), jnp.float32)
    pack(main, tail, staged)
    away_ref[...] = staged[...].astype(jnp.bfloat16).reshape(LANES, SHARE, 128)


def pair_kernel(main_ref, tail_ref, other_ref, shares_ref, main, tail, staged):
    main[...] = main_ref[...]
    tail[:C] = tail_ref[...]
    tail[C:] = jnp.zeros((TAIL - C, 128), jnp.float32)
    pack(main, tail, staged)
    total = staged[...].reshape(LANES, SHARE, 128) + other_ref[...].astype(jnp.float32)
    shares_ref[...] = total.astype(jnp.bfloat16)


def total_kernel(shares_ref, gradient_ref, tail):
    group = lax.broadcasted_iota(jnp.int32, (3, 128), 1) // 32
    ends = []
    for quarter in range(4):
        for core in range(2):
            acc = None
            for k in range(16):
                y, z, x = quarter // 2 + 2 * (k // 8), quarter % 2 + 2 * (k // 2 % 4), k % 2
                lane = ((y * 8 + z) * 2 + x) * 2 + core
                term = shares_ref[lane].astype(jnp.float32)
                acc = term if acc is None else acc + term
            at = 128 * (2 * quarter + core)
            gradient_ref[:, 0, at : at + 128] = acc[:10]
            ends.append(acc[10:13])
    for block in range(2):
        for q in range(4):
            row = None
            for g in range(4):
                end = ends[4 * block + g]
                end = end if g == q else pltpu.roll(end, (32 * (g - q)) % 128, 1)
                row = end if row is None else jnp.where(group == g, end, row)
            tail[pl.ds(q, 3, 4)] = row
        at = 1024 + 128 * block
        gradient_ref[:, 0, at : at + 128] = tail[:10]


def partner(y, z, core, t):
    y = ((y + core) % 4 ^ 1) - core if t & 2 else y
    z = ((z + core) % 8 ^ 1) - core if t & 1 else z
    return ((y % 4) * 8 + z % 8) * 2 + core


def squares():
    groups = []
    for x in range(2):
        for core in range(2):
            for y in range(0, 4, 2):
                for z in range(0, 8, 2):
                    group = []
                    for section in range(2):
                        for quarter in range(4):
                            near = (y + core + (quarter // 2 + core) % 2) % 4
                            side = (z + core + (quarter % 2 + core) % 2) % 8
                            group.append((((section * 4 + near) * 8 + side) * 2 + x) * 2 + core)
                    groups.append(group)
    return groups


def exchange(block, t, moves):
    at = [(y, z, core) for y in range(4) for z in range(8) for core in range(2)]
    route = [
        (64 * source + partner(*place, 0), 64 * target + partner(*place, t))
        for source, target in moves
        for place in at
    ]
    return lax.ppermute(block, ("section", "y", "z", "core"), route)


def local(inputs, weights, gains, timesteps, text_pooled):
    half = jax.ShapeDtypeStruct((ROWS, C), jnp.bfloat16)
    whole = jax.ShapeDtypeStruct(inputs.shape, jnp.bfloat16)
    sent_0, sent_1, active_0, active_1, condition, weight = pl.pallas_call(
        down_kernel,
        out_shape=(half,) * 4
        + (
            jax.ShapeDtypeStruct((MICRO, 1, C), jnp.float32),
            jax.ShapeDtypeStruct((C, C), jnp.bfloat16),
        ),
        in_specs=[HBM] * 5,
        out_specs=(VMEM,) * 6,
        scratch_shapes=[
            pltpu.SMEM(timesteps.shape, jnp.int32),
            pltpu.VMEM(inputs.shape[1:], jnp.bfloat16),
            pltpu.VMEM(gains.shape, jnp.float32),
            pltpu.VMEM(text_pooled.shape, jnp.bfloat16),
            pltpu.SemaphoreType.DMA((5,)),
        ],
        compiler_params=WHOLE,
    )(timesteps, inputs, weights, gains, text_pooled)
    sent, first_active = (sent_0, sent_1), (active_0, active_1)
    received = [lax.ppermute(rows, "section", [(0, 1)]) for rows in sent]
    both = jax.ShapeDtypeStruct((MICRO * ROWS, C), jnp.bfloat16)
    piece = jax.ShapeDtypeStruct((PIECE, 128), jnp.bfloat16)
    slots = jax.ShapeDtypeStruct((8, PIECE, 128), jnp.bfloat16)

    def up(number, more, specs, *before):
        return pl.pallas_call(
            functools.partial(up_kernel, number),
            out_shape=(whole, both) + more,
            in_specs=[VMEM, VMEM, HBM, VMEM, VMEM] + [HBM] * (2 + 2 * number),
            out_specs=(HBM, HBM) + specs,
            scratch_shapes=[
                pltpu.VMEM((ROWS, C), jnp.bfloat16),
                pltpu.VMEM((ROWS, C), jnp.bfloat16),
                pltpu.VMEM((8, PIECE, 128), jnp.bfloat16),
                pltpu.VMEM((ROWS, C), jnp.bfloat16),
                pltpu.SemaphoreType.DMA((5,)),
            ],
            input_output_aliases={7: 0, 8: 1} if number else {},
            compiler_params=MOST,
            cost_estimate=pl.CostEstimate(
                flops=2_000_000_000, bytes_accessed=4_000_000, transcendentals=0
            ),
        )(
            condition, received[number], inputs, weight, gains, sent[number],
            first_active[number], *before,
        )

    outs, actives, *cots, back = up(0, (piece,) * 4 + (half,), (VMEM,) * 5)
    returned = lax.ppermute(back, "section", [(1, 0)])
    outs, actives, pieces = up(1, (slots,), (HBM,), outs, actives)
    pieces = pl.pallas_call(
        returned_kernel,
        out_shape=slots,
        in_specs=[VMEM, HBM],
        out_specs=HBM,
        scratch_shapes=[pltpu.VMEM((4, PIECE, 128), jnp.bfloat16), pltpu.SemaphoreType.DMA],
        input_output_aliases={1: 0},
        compiler_params=MOST,
        cost_estimate=pl.CostEstimate(flops=COST, bytes_accessed=2_000_000, transcendentals=0),
    )(returned, pieces)
    others = [exchange(actives, t, ((0, 0), (1, 1))) for t in range(1, 4)]
    turned = [exchange(cots[t], t, ((1, 1),)) for t in range(1, 4)]
    arrived = lax.all_to_all(
        pieces, ("section",) + DP, 0, 0, axis_index_groups=squares(), tiled=True
    )
    packed = [
        pltpu.VMEM((C, 128), jnp.float32),
        pltpu.VMEM((TAIL, 128), jnp.float32),
        pltpu.VMEM((LANES * SHARE, 128), jnp.float32),
    ]
    share = jax.ShapeDtypeStruct((LANES, SHARE, 128), jnp.bfloat16)
    gathered = pl.pallas_call(
        gathered_kernel,
        out_shape=jax.ShapeDtypeStruct((8, 128), jnp.float32),
        in_specs=[HBM] * 3,
        out_specs=VMEM,
        compiler_params=PARAMS,
        cost_estimate=pl.CostEstimate(flops=COST, bytes_accessed=2_000_000, transcendentals=0),
    )(*others)
    main, tail, away = pl.pallas_call(
        weight_kernel,
        out_shape=(jax.ShapeDtypeStruct((C, 128), jnp.float32),) * 2 + (share,),
        in_specs=[VMEM] * 9 + [HBM],
        out_specs=(VMEM,) * 3,
        scratch_shapes=packed,
        compiler_params=PARAMS,
    )(actives, *others, arrived, cots[0], *turned, gathered)
    other = lax.ppermute(away, "core", [(0, 1), (1, 0)])
    shares = pl.pallas_call(
        pair_kernel,
        out_shape=share,
        in_specs=[VMEM] * 3,
        out_specs=VMEM,
        scratch_shapes=packed,
        compiler_params=PARAMS,
    )(main, tail, other)
    shares = lax.all_to_all(shares, DP, 0, 0, tiled=True)
    gradient = pl.pallas_call(
        total_kernel,
        out_shape=jax.ShapeDtypeStruct((C // LANES, 1, C), jnp.float32),
        in_specs=[VMEM],
        out_specs=VMEM,
        scratch_shapes=[pltpu.VMEM((12, 128), jnp.float32)],
        compiler_params=PARAMS,
    )(shares)
    return (outs, jnp.transpose(gradient, (1, 0, 2)))


def solution(mesh):
    fine = Mesh(mesh.devices.reshape(2, 4, 8, 2, 2), ("section",) + DP)
    return jax.shard_map(
        local,
        mesh=fine,
        in_specs=(
            P("section", None, DP, None),
            P("section", None, None),
            P("section", None),
            P(),
            P(),
        ),
        out_specs=(P("section", None, DP, None), P("section", DP, None)),
        check_vma=False,
    )
```

```python
import functools
import math

import jax
import jax.numpy as jnp
from jax import lax
from jax.experimental import pallas as pl
from jax.experimental.pallas import tpu as pltpu
from jax.sharding import Mesh, PartitionSpec as P

PIX = 1024
MICRO = 2
ROWS = 128
LANES = 128
C = 1280
DP = ("y", "z", "x", "core")
COST = 50_000_000_000
PIECE = 320
SHARE = 16
TAIL = C + 8
PARAMS = pltpu.CompilerParams(vmem_limit_bytes=40 * 1024 * 1024)
WHOLE = pltpu.CompilerParams(vmem_limit_bytes=52 * 1024 * 1024)
MOST = pltpu.CompilerParams(vmem_limit_bytes=51 * 1024 * 1024)
VMEM = pl.BlockSpec(memory_space=pltpu.VMEM)
HBM = pl.BlockSpec(memory_space=pltpu.HBM)


def condition_row(steps_ref, text_ref, number):
    latent = lax.axis_index(DP) * ROWS // PIX
    step = steps_ref[number, latent].astype(jnp.float32)
    lane = lax.broadcasted_iota(jnp.int32, (1, C), 1)
    index = jnp.where(lane < C // 2, lane, lane - C // 2).astype(jnp.float32)
    angle = step * jnp.exp(-math.log(10000.0) * index / (C // 2))
    waves = jnp.where(lane < C // 2, jnp.cos(angle), jnp.sin(angle))
    text = text_ref[number].astype(jnp.float32)
    mine = lax.broadcasted_iota(jnp.int32, text.shape, 0) == latent
    return waves + jnp.sum(jnp.where(mine, text, 0.0), axis=0, keepdims=True)


def normed_rows(hidden, condition, gain):
    shifted = hidden + condition
    inverse = lax.rsqrt(jnp.mean(shifted * shifted, axis=-1, keepdims=True) + 1e-05)
    normed = shifted * inverse * gain
    sigma = 1.0 / (1.0 + jnp.exp(-normed))
    return shifted, inverse, normed, sigma


def down_kernel(
    steps_hbm, rows_hbm, weight_hbm, gain_hbm, text_hbm,
    sent_0, sent_1, active_0, active_1, cond_ref, weight_ref,
    steps_ref, rows_ref, gain_ref, text_ref, sems,
):
    copies = [
        pltpu.make_async_copy(source, target, sems.at[at])
        for at, (source, target) in enumerate(
            (
                (steps_hbm, steps_ref),
                (text_hbm, text_ref),
                (rows_hbm.at[0], rows_ref),
                (gain_hbm, gain_ref),
                (weight_hbm.at[0], weight_ref),
            )
        )
    ]
    for copy in copies:
        copy.start()
    copies[0].wait()
    copies[1].wait()
    for number in range(MICRO):
        cond_ref[number] = condition_row(steps_ref, text_ref, number)
    copies[2].wait()
    copies[3].wait()
    for number, sent_ref, active_ref in ((0, sent_0, active_0), (1, sent_1, active_1)):
        hidden = rows_ref[number].astype(jnp.float32)
        _, _, normed, sigma = normed_rows(hidden, cond_ref[number], gain_ref[...])
        active = (normed * sigma).astype(jnp.bfloat16)
        active_ref[...] = active
        if number == 0:
            copies[4].wait()
        result = hidden + jnp.dot(active, weight_ref[...], preferred_element_type=jnp.float32)
        sent_ref[...] = result.astype(jnp.bfloat16)


def own_quarter():
    return 2 * lax.rem(lax.axis_index("y"), 2) + lax.rem(lax.axis_index("z"), 2)


def store_pieces(pieces_ref, first, values):
    half = ROWS // 2
    low = lax.broadcasted_iota(jnp.int32, (half, 128), 1) < 64
    rounded = values.astype(jnp.bfloat16)
    for quarter in range(4):
        slot = first + quarter
        pieces_ref[slot, :ROWS] = rounded[:, 256 * quarter : 256 * quarter + 128]
        pieces_ref[slot, ROWS : 2 * ROWS] = rounded[:, 256 * quarter + 128 : 256 * quarter + 256]
        at = 1024 + 128 * (quarter // 2)
        block = values[:, at : at + 128]
        turned = pltpu.roll(block, 64, 1)
        top, bottom = (block, turned) if quarter % 2 == 0 else (turned, block)
        pieces_ref[slot, 2 * ROWS :] = jnp.where(low, top[:half], bottom[half:]).astype(
            jnp.bfloat16
        )


def up_kernel(number, *refs):
    cond_ref, arrived_ref, rows_hbm, weight_ref, gain_ref, sent_hbm, first_active_hbm = refs[:7]
    outs_hbm, actives_hbm, cot_ref, back_ref = refs[7 + 2 * number : -4]
    out_ref, active_ref, rows_ref, sems = refs[-4:]
    active_hbm = actives_hbm.at[pl.ds(ROWS * number, ROWS)]
    rows_copy = pltpu.make_async_copy(rows_hbm.at[0, number], rows_ref, sems.at[0])
    rows_copy.start()
    down = lax.axis_index("section") == 0
    kept = [
        pltpu.make_async_copy(sent_hbm, outs_hbm.at[0, number], sems.at[1]),
        pltpu.make_async_copy(first_active_hbm, active_hbm, sems.at[2]),
    ]
    made = [
        pltpu.make_async_copy(out_ref, outs_hbm.at[0, number], sems.at[1]),
        pltpu.make_async_copy(active_ref, active_hbm, sems.at[2]),
    ]

    @pl.when(down)
    def _():
        for copy in kept:
            copy.start()

    gain = gain_ref[...]
    hidden = arrived_ref[...].astype(jnp.float32)
    shifted, inverse, normed, sigma = normed_rows(hidden, cond_ref[number], gain)
    active = (normed * sigma).astype(jnp.bfloat16)
    active_ref[...] = active
    weight = weight_ref[...]
    upper = hidden + jnp.dot(active, weight, preferred_element_type=jnp.float32)
    out_ref[...] = upper.astype(jnp.bfloat16)

    @pl.when(jnp.logical_not(down))
    def _():
        for copy in made:
            copy.start()

    rows_copy.wait()
    cot = (upper - rows_ref[...].astype(jnp.float32)) / math.sqrt(MICRO * ROWS * LANES)
    cot = cot.astype(jnp.bfloat16)
    cot_ref[...] = cot
    through = lax.dot_general(
        cot, weight, (((1,), (1,)), ((), ())), preferred_element_type=jnp.float32
    )
    scaled = through * sigma * (1.0 + normed * (1.0 - sigma)) * gain
    inner = jnp.mean(scaled * shifted, axis=-1, keepdims=True)
    back = cot.astype(jnp.float32) + inverse * scaled - shifted * inverse**3 * inner
    back_ref[...] = back.astype(jnp.bfloat16)

    @pl.when(down)
    def _():
        for copy in kept:
            copy.wait()

    @pl.when(jnp.logical_not(down))
    def _():
        for copy in made:
            copy.wait()


def pack(main, tail, staged):
    group = lax.broadcasted_iota(jnp.int32, (3, 128), 1) // 32
    staged[...] = jnp.zeros_like(staged)

    def lanes(block, carry):
        base = pl.multiple_of(block * 80, 80)
        to = pl.multiple_of(block * 8 * SHARE, 8 * SHARE)
        for lane in range(8):
            at, put = base + 10 * lane, to + SHARE * lane
            staged[pl.ds(put, 10)] = main[pl.ds(at, 10)]
            row = tail[pl.ds(at, 3, 4)]
            for q in range(1, 4):
                row = jnp.where(group == q, tail[pl.ds(at + q, 3, 4)], row)
            staged[pl.ds(put + 10, 3)] = row
        return carry

    lax.fori_loop(0, LANES // 8, lanes, 0)


def pieces_kernel(returned_ref, cot_ref, back_ref, pieces_hbm, pieces_ref, sems):
    copies = [
        pltpu.make_async_copy(pieces_ref.at[pl.ds(at, 4)], pieces_hbm.at[pl.ds(at, 4)], sem)
        for at, sem in ((0, sems.at[0]), (4, sems.at[1]))
    ]
    store_pieces(pieces_ref, 4, cot_ref[...].astype(jnp.float32))
    copies[1].start()
    down = lax.axis_index("section") == 0
    rows = jnp.where(down, returned_ref[...], back_ref[...])
    store_pieces(pieces_ref, 0, rows.astype(jnp.float32))
    copies[0].start()
    for copy in copies:
        copy.wait()


def cots_kernel(cot_ref, pieces_hbm, *refs):
    del pieces_hbm
    store_pieces(refs[3], 0, cot_ref[...].astype(jnp.float32))
    own = own_quarter()
    for turn in range(1, 4):
        refs[turn - 1][...] = refs[3][lax.bitwise_xor(own, turn)]


def own_kernel(cot_ref, *refs):
    own_ref, pieces_ref = refs[3:]
    store_pieces(pieces_ref, 0, cot_ref[...].astype(jnp.float32))
    own_ref[...] = pieces_ref[own_quarter()]


def weight_kernel(*refs):
    active_refs, piece_ref, cot_refs = refs[:4], refs[4], refs[5:9]
    main_ref, tail_ref, away_ref, main, tail, staged = refs[9:]
    down, core = lax.axis_index("section") == 0, lax.axis_index("core")
    own = own_quarter()
    low = lax.broadcasted_iota(jnp.int32, (ROWS // 2, 128), 1) < 64
    zero = jnp.zeros((ROWS // 2, 128), jnp.bfloat16)
    product = None
    for turn in range(4):
        right = []
        for number in range(MICRO):
            piece = piece_ref[4 * number + lax.bitwise_xor(own, turn)]
            if number == 0:
                piece = jnp.where(down, piece, cot_refs[turn][...])
            end = piece[2 * ROWS :]
            right.append(
                jnp.concatenate(
                    [
                        piece[:ROWS],
                        piece[ROWS : 2 * ROWS],
                        jnp.concatenate([jnp.where(low, end, zero), jnp.where(low, zero, end)]),
                    ],
                    axis=1,
                )
            )
        term = lax.dot_general(
            active_refs[turn][...], jnp.concatenate(right), (((0,), (0,)), ((), ())),
            preferred_element_type=jnp.float32,
        )
        product = term if product is None else product + term
    first, second = product[:, :128], product[:, 128:256]
    both = product[:, 256:] + pltpu.roll(product[:, 256:], 64, 1)
    turned = pltpu.roll(both, 32, 1)
    even = (lax.broadcasted_iota(jnp.int32, both.shape, 1) // 32) % 2 == 0
    lower, upper = jnp.where(even, both, turned), jnp.where(even, turned, both)
    zeroth = core == 0
    main_ref[...] = jnp.where(zeroth, first, second)
    tail_ref[...] = jnp.where(zeroth, lower, upper)
    main[...] = jnp.where(zeroth, second, first)
    tail[:C] = jnp.where(zeroth, upper, lower)
    tail[C:] = jnp.zeros((TAIL - C, 128), jnp.float32)
    pack(main, tail, staged)
    away_ref[...] = staged[...].astype(jnp.bfloat16).reshape(LANES, SHARE, 128)


def pair_kernel(main_ref, tail_ref, other_ref, shares_ref, main, tail, staged):
    main[...] = main_ref[...]
    tail[:C] = tail_ref[...]
    tail[C:] = jnp.zeros((TAIL - C, 128), jnp.float32)
    pack(main, tail, staged)
    total = staged[...].reshape(LANES, SHARE, 128) + other_ref[...].astype(jnp.float32)
    shares_ref[...] = total.astype(jnp.bfloat16)


def total_kernel(shares_ref, gradient_ref, tail):
    group = lax.broadcasted_iota(jnp.int32, (3, 128), 1) // 32
    ends = []
    for quarter in range(4):
        for core in range(2):
            acc = None
            for k in range(16):
                y, z, x = quarter // 2 + 2 * (k // 8), quarter % 2 + 2 * (k // 2 % 4), k % 2
                lane = ((y * 8 + z) * 2 + x) * 2 + core
                term = shares_ref[lane].astype(jnp.float32)
                acc = term if acc is None else acc + term
            at = 128 * (2 * quarter + core)
            gradient_ref[:, 0, at : at + 128] = acc[:10]
            ends.append(acc[10:13])
    for block in range(2):
        for q in range(4):
            row = None
            for g in range(4):
                end = ends[4 * block + g]
                end = end if g == q else pltpu.roll(end, (32 * (g - q)) % 128, 1)
                row = end if row is None else jnp.where(group == g, end, row)
            tail[pl.ds(q, 3, 4)] = row
        at = 1024 + 128 * block
        gradient_ref[:, 0, at : at + 128] = tail[:10]


def partner(y, z, core, t):
    y = ((y + core) % 4 ^ 1) - core if t & 2 else y
    z = ((z + core) % 8 ^ 1) - core if t & 1 else z
    return ((y % 4) * 8 + z % 8) * 2 + core


def squares():
    groups = []
    for x in range(2):
        for core in range(2):
            for y in range(0, 4, 2):
                for z in range(0, 8, 2):
                    group = []
                    for section in range(2):
                        for quarter in range(4):
                            near = (y + core + (quarter // 2 + core) % 2) % 4
                            side = (z + core + (quarter % 2 + core) % 2) % 8
                            group.append((((section * 4 + near) * 8 + side) * 2 + x) * 2 + core)
                    groups.append(group)
    return groups


def exchange(block, t, moves):
    at = [(y, z, core) for y in range(4) for z in range(8) for core in range(2)]
    route = [
        (64 * source + partner(*place, 0), 64 * target + partner(*place, t))
        for source, target in moves
        for place in at
    ]
    return lax.ppermute(block, ("section", "y", "z", "core"), route)


def local(inputs, weights, gains, timesteps, text_pooled):
    half = jax.ShapeDtypeStruct((ROWS, C), jnp.bfloat16)
    whole = jax.ShapeDtypeStruct(inputs.shape, jnp.bfloat16)
    sent_0, sent_1, active_0, active_1, condition, weight = pl.pallas_call(
        down_kernel,
        out_shape=(half,) * 4
        + (
            jax.ShapeDtypeStruct((MICRO, 1, C), jnp.float32),
            jax.ShapeDtypeStruct((C, C), jnp.bfloat16),
        ),
        in_specs=[HBM] * 5,
        out_specs=(VMEM,) * 6,
        scratch_shapes=[
            pltpu.SMEM(timesteps.shape, jnp.int32),
            pltpu.VMEM(inputs.shape[1:], jnp.bfloat16),
            pltpu.VMEM(gains.shape, jnp.float32),
            pltpu.VMEM(text_pooled.shape, jnp.bfloat16),
            pltpu.SemaphoreType.DMA((5,)),
        ],
        compiler_params=WHOLE,
    )(timesteps, inputs, weights, gains, text_pooled)
    sent, first_active = (sent_0, sent_1), (active_0, active_1)
    received = [lax.ppermute(rows, "section", [(0, 1)]) for rows in sent]
    both = jax.ShapeDtypeStruct((MICRO * ROWS, C), jnp.bfloat16)
    piece = jax.ShapeDtypeStruct((PIECE, 128), jnp.bfloat16)
    slots = jax.ShapeDtypeStruct((8, PIECE, 128), jnp.bfloat16)

    def up(number, *before):
        return pl.pallas_call(
            functools.partial(up_kernel, number),
            out_shape=(whole, both, half, half),
            in_specs=[VMEM, VMEM, HBM, VMEM, VMEM] + [HBM] * (2 + 2 * number),
            out_specs=(HBM, HBM, VMEM, VMEM),
            scratch_shapes=[
                pltpu.VMEM((ROWS, C), jnp.bfloat16),
                pltpu.VMEM((ROWS, C), jnp.bfloat16),
                pltpu.VMEM((ROWS, C), jnp.bfloat16),
                pltpu.SemaphoreType.DMA((3,)),
            ],
            input_output_aliases={7: 0, 8: 1} if number else {},
            compiler_params=MOST,
            cost_estimate=pl.CostEstimate(
                flops=2_000_000_000, bytes_accessed=4_000_000, transcendentals=0
            ),
        )(
            condition, received[number], inputs, weight, gains, sent[number],
            first_active[number], *before,
        )

    outs, actives, cot_0, back_0 = up(0)
    returned = lax.ppermute(back_0, "section", [(1, 0)])
    outs, actives, cot_1, back_1 = up(1, outs, actives)
    pieces = pl.pallas_call(
        pieces_kernel,
        out_shape=slots,
        in_specs=[VMEM] * 3,
        out_specs=HBM,
        scratch_shapes=[
            pltpu.VMEM((8, PIECE, 128), jnp.bfloat16),
            pltpu.SemaphoreType.DMA((2,)),
        ],
        compiler_params=MOST,
        cost_estimate=pl.CostEstimate(flops=COST, bytes_accessed=2_000_000, transcendentals=0),
    )(returned, cot_1, back_1)
    cots = pl.pallas_call(
        cots_kernel,
        out_shape=(piece,) * 3,
        in_specs=[VMEM, HBM],
        out_specs=(VMEM,) * 3,
        scratch_shapes=[pltpu.VMEM((4, PIECE, 128), jnp.bfloat16)],
        compiler_params=PARAMS,
    )(cot_0, pieces)
    others = [exchange(actives, t, ((0, 0), (1, 1))) for t in range(1, 4)]
    turned = [exchange(cots[t - 1], t, ((1, 1),)) for t in range(1, 4)]
    arrived = lax.all_to_all(
        pieces, ("section",) + DP, 0, 0, axis_index_groups=squares(), tiled=True
    )
    packed = [
        pltpu.VMEM((C, 128), jnp.float32),
        pltpu.VMEM((TAIL, 128), jnp.float32),
        pltpu.VMEM((LANES * SHARE, 128), jnp.float32),
    ]
    share = jax.ShapeDtypeStruct((LANES, SHARE, 128), jnp.bfloat16)
    own = pl.pallas_call(
        own_kernel,
        out_shape=piece,
        in_specs=[VMEM] + [HBM] * 3,
        out_specs=VMEM,
        scratch_shapes=[pltpu.VMEM((4, PIECE, 128), jnp.bfloat16)],
        compiler_params=PARAMS,
        cost_estimate=pl.CostEstimate(flops=COST, bytes_accessed=2_000_000, transcendentals=0),
    )(cot_0, *others)
    main, tail, away = pl.pallas_call(
        weight_kernel,
        out_shape=(jax.ShapeDtypeStruct((C, 128), jnp.float32),) * 2 + (share,),
        in_specs=[VMEM] * 9,
        out_specs=(VMEM,) * 3,
        scratch_shapes=packed,
        compiler_params=PARAMS,
    )(actives, *others, arrived, own, *turned)
    other = lax.ppermute(away, "core", [(0, 1), (1, 0)])
    shares = pl.pallas_call(
        pair_kernel,
        out_shape=share,
        in_specs=[VMEM] * 3,
        out_specs=VMEM,
        scratch_shapes=packed,
        compiler_params=PARAMS,
    )(main, tail, other)
    shares = lax.all_to_all(shares, DP, 0, 0, tiled=True)
    gradient = pl.pallas_call(
        total_kernel,
        out_shape=jax.ShapeDtypeStruct((C // LANES, 1, C), jnp.float32),
        in_specs=[VMEM],
        out_specs=VMEM,
        scratch_shapes=[pltpu.VMEM((12, 128), jnp.float32)],
        compiler_params=PARAMS,
    )(shares)
    return (outs, jnp.transpose(gradient, (1, 0, 2)))


def solution(mesh):
    fine = Mesh(mesh.devices.reshape(2, 4, 8, 2, 2), ("section",) + DP)
    return jax.shard_map(
        local,
        mesh=fine,
        in_specs=(
            P("section", None, DP, None),
            P("section", None, None),
            P("section", None),
            P(),
            P(),
        ),
        out_specs=(P("section", None, DP, None), P("section", DP, None)),
        check_vma=False,
    )
```

```python
import functools
import math

import jax
import jax.numpy as jnp
from jax import lax
from jax.experimental import pallas as pl
from jax.experimental.pallas import tpu as pltpu
from jax.sharding import Mesh, PartitionSpec as P

PIX = 1024
MICRO = 2
ROWS = 128
LANES = 128
C = 1280
DP = ("y", "z", "x", "core")
COST = 50_000_000_000
PIECE = 320
SHARE = 16
TAIL = C + 48
PARAMS = pltpu.CompilerParams(vmem_limit_bytes=40 * 1024 * 1024)
WHOLE = pltpu.CompilerParams(vmem_limit_bytes=52 * 1024 * 1024)
MOST = pltpu.CompilerParams(vmem_limit_bytes=51 * 1024 * 1024)
VMEM = pl.BlockSpec(memory_space=pltpu.VMEM)
HBM = pl.BlockSpec(memory_space=pltpu.HBM)


def condition_row(steps_ref, text_ref, number):
    latent = lax.axis_index(DP) * ROWS // PIX
    step = steps_ref[number, latent].astype(jnp.float32)
    lane = lax.broadcasted_iota(jnp.int32, (1, C), 1)
    index = jnp.where(lane < C // 2, lane, lane - C // 2).astype(jnp.float32)
    angle = step * jnp.exp(-math.log(10000.0) * index / (C // 2))
    waves = jnp.where(lane < C // 2, jnp.cos(angle), jnp.sin(angle))
    text = text_ref[number].astype(jnp.float32)
    mine = lax.broadcasted_iota(jnp.int32, text.shape, 0) == latent
    return waves + jnp.sum(jnp.where(mine, text, 0.0), axis=0, keepdims=True)


def normed_rows(hidden, condition, gain):
    shifted = hidden + condition
    inverse = lax.rsqrt(jnp.mean(shifted * shifted, axis=-1, keepdims=True) + 1e-05)
    normed = shifted * inverse * gain
    sigma = 1.0 / (1.0 + jnp.exp(-normed))
    return shifted, inverse, normed, sigma


def down_kernel(
    steps_hbm, rows_hbm, weight_hbm, gain_hbm, text_hbm,
    sent_0, sent_1, active_0, active_1, cond_ref, weight_ref,
    steps_ref, rows_ref, gain_ref, text_ref, sems,
):
    copies = [
        pltpu.make_async_copy(source, target, sems.at[at])
        for at, (source, target) in enumerate(
            (
                (steps_hbm, steps_ref),
                (text_hbm, text_ref),
                (rows_hbm.at[0], rows_ref),
                (gain_hbm, gain_ref),
                (weight_hbm.at[0], weight_ref),
            )
        )
    ]
    for copy in copies:
        copy.start()
    copies[0].wait()
    copies[1].wait()
    for number in range(MICRO):
        cond_ref[number] = condition_row(steps_ref, text_ref, number)
    copies[2].wait()
    copies[3].wait()
    for number, sent_ref, active_ref in ((0, sent_0, active_0), (1, sent_1, active_1)):
        hidden = rows_ref[number].astype(jnp.float32)
        _, _, normed, sigma = normed_rows(hidden, cond_ref[number], gain_ref[...])
        active = (normed * sigma).astype(jnp.bfloat16)
        active_ref[...] = active
        if number == 0:
            copies[4].wait()
        result = hidden + jnp.dot(active, weight_ref[...], preferred_element_type=jnp.float32)
        sent_ref[...] = result.astype(jnp.bfloat16)


def own_quarter():
    return 2 * lax.rem(lax.axis_index("y"), 2) + lax.rem(lax.axis_index("z"), 2)


def store_pieces(pieces_ref, first, values):
    half = ROWS // 2
    low = lax.broadcasted_iota(jnp.int32, (half, 128), 1) < 64
    rounded = values.astype(jnp.bfloat16)
    for quarter in range(4):
        slot = first + quarter
        pieces_ref[slot, :ROWS] = rounded[:, 256 * quarter : 256 * quarter + 128]
        pieces_ref[slot, ROWS : 2 * ROWS] = rounded[:, 256 * quarter + 128 : 256 * quarter + 256]
        at = 1024 + 128 * (quarter // 2)
        block = values[:, at : at + 128]
        turned = pltpu.roll(block, 64, 1)
        top, bottom = (block, turned) if quarter % 2 == 0 else (turned, block)
        pieces_ref[slot, 2 * ROWS :] = jnp.where(low, top[:half], bottom[half:]).astype(
            jnp.bfloat16
        )


def up_kernel(number, *refs):
    cond_ref, arrived_ref, rows_hbm, weight_ref, gain_ref, sent_hbm, first_active_hbm = refs[:7]
    outs_hbm, actives_hbm, cot_ref, back_ref = refs[7 + 2 * number : -4]
    out_ref, active_ref, rows_ref, sems = refs[-4:]
    active_hbm = actives_hbm.at[pl.ds(ROWS * number, ROWS)]
    rows_copy = pltpu.make_async_copy(rows_hbm.at[0, number], rows_ref, sems.at[0])
    rows_copy.start()
    down = lax.axis_index("section") == 0
    kept = [
        pltpu.make_async_copy(sent_hbm, outs_hbm.at[0, number], sems.at[1]),
        pltpu.make_async_copy(first_active_hbm, active_hbm, sems.at[2]),
    ]
    made = [
        pltpu.make_async_copy(out_ref, outs_hbm.at[0, number], sems.at[1]),
        pltpu.make_async_copy(active_ref, active_hbm, sems.at[2]),
    ]

    @pl.when(down)
    def _():
        for copy in kept:
            copy.start()

    gain = gain_ref[...]
    hidden = arrived_ref[...].astype(jnp.float32)
    shifted, inverse, normed, sigma = normed_rows(hidden, cond_ref[number], gain)
    active = (normed * sigma).astype(jnp.bfloat16)
    active_ref[...] = active
    weight = weight_ref[...]
    upper = hidden + jnp.dot(active, weight, preferred_element_type=jnp.float32)
    out_ref[...] = upper.astype(jnp.bfloat16)

    @pl.when(jnp.logical_not(down))
    def _():
        for copy in made:
            copy.start()

    rows_copy.wait()
    cot = (upper - rows_ref[...].astype(jnp.float32)) / math.sqrt(MICRO * ROWS * LANES)
    cot = cot.astype(jnp.bfloat16)
    cot_ref[...] = cot
    through = lax.dot_general(
        cot, weight, (((1,), (1,)), ((), ())), preferred_element_type=jnp.float32
    )
    scaled = through * sigma * (1.0 + normed * (1.0 - sigma)) * gain
    inner = jnp.mean(scaled * shifted, axis=-1, keepdims=True)
    back = cot.astype(jnp.float32) + inverse * scaled - shifted * inverse**3 * inner
    back_ref[...] = back.astype(jnp.bfloat16)

    @pl.when(down)
    def _():
        for copy in kept:
            copy.wait()

    @pl.when(jnp.logical_not(down))
    def _():
        for copy in made:
            copy.wait()


def pack(main, tail, staged):
    group = lax.broadcasted_iota(jnp.int32, (3, 128), 1) // 32
    staged[...] = jnp.zeros_like(staged)

    def lanes(block, carry):
        base = pl.multiple_of(block * 80, 80)
        to = pl.multiple_of(block * 8 * SHARE, 8 * SHARE)
        for lane in range(8):
            at, put = base + 10 * lane, to + SHARE * lane
            staged[pl.ds(put, 10)] = main[pl.ds(at, 10)]
            row = tail[pl.ds(at, 3, 4)]
            for q in range(1, 4):
                row = jnp.where(group == q, tail[pl.ds(at + q, 3, 4)], row)
            staged[pl.ds(put + 10, 3)] = row
        return carry

    lax.fori_loop(0, LANES // 8, lanes, 0)


def pieces_kernel(returned_ref, cot_ref, back_ref, pieces_hbm, pieces_ref, sems):
    copies = [
        pltpu.make_async_copy(pieces_ref.at[pl.ds(at, 4)], pieces_hbm.at[pl.ds(at, 4)], sem)
        for at, sem in ((0, sems.at[0]), (4, sems.at[1]))
    ]
    store_pieces(pieces_ref, 4, cot_ref[...].astype(jnp.float32))
    copies[1].start()
    down = lax.axis_index("section") == 0
    rows = jnp.where(down, returned_ref[...], back_ref[...])
    store_pieces(pieces_ref, 0, rows.astype(jnp.float32))
    copies[0].start()
    for copy in copies:
        copy.wait()


def cots_kernel(cot_ref, pieces_hbm, *refs):
    del pieces_hbm
    store_pieces(refs[3], 0, cot_ref[...].astype(jnp.float32))
    own = own_quarter()
    for turn in range(1, 4):
        refs[turn - 1][...] = refs[3][lax.bitwise_xor(own, turn)]


def own_kernel(cot_ref, *refs):
    own_ref, pieces_ref = refs[3:]
    store_pieces(pieces_ref, 0, cot_ref[...].astype(jnp.float32))
    own_ref[...] = pieces_ref[own_quarter()]


def weight_kernel(*refs):
    active_refs, piece_ref, cot_refs = refs[:4], refs[4], refs[5:9]
    main_ref, tail_ref, away_ref, main, tail, staged = refs[9:]
    down, core = lax.axis_index("section") == 0, lax.axis_index("core")
    own = own_quarter()
    low = lax.broadcasted_iota(jnp.int32, (ROWS // 2, 128), 1) < 64
    zero = jnp.zeros((ROWS // 2, 128), jnp.bfloat16)
    product = None
    for turn in range(4):
        right = []
        for number in range(MICRO):
            piece = piece_ref[4 * number + lax.bitwise_xor(own, turn)]
            if number == 0:
                piece = jnp.where(down, piece, cot_refs[turn][...])
            end = piece[2 * ROWS :]
            right.append(
                jnp.concatenate(
                    [
                        piece[:ROWS],
                        piece[ROWS : 2 * ROWS],
                        jnp.concatenate([jnp.where(low, end, zero), jnp.where(low, zero, end)]),
                    ],
                    axis=1,
                )
            )
        term = lax.dot_general(
            active_refs[turn][...], jnp.concatenate(right), (((0,), (0,)), ((), ())),
            preferred_element_type=jnp.float32,
        )
        product = term if product is None else product + term
    first, second = product[:, :128], product[:, 128:256]
    both = product[:, 256:] + pltpu.roll(product[:, 256:], 64, 1)
    turned = pltpu.roll(both, 32, 1)
    even = (lax.broadcasted_iota(jnp.int32, both.shape, 1) // 32) % 2 == 0
    lower, upper = jnp.where(even, both, turned), jnp.where(even, turned, both)
    zeroth = core == 0
    main_ref[...] = jnp.where(zeroth, first, second)
    tail_ref[...] = jnp.where(zeroth, lower, upper)
    main[:C] = jnp.where(zeroth, second, first)
    tail[:C] = jnp.where(zeroth, upper, lower)
    tail[C:] = jnp.zeros((TAIL - C, 128), jnp.float32)
    pack(main, tail, staged)
    away_ref[...] = staged[: LANES * SHARE].astype(jnp.bfloat16).reshape(LANES, SHARE, 128)


def pair_kernel(main_ref, tail_ref, other_ref, shares_ref, main, tail, staged):
    main[:C] = main_ref[...]
    tail[:C] = tail_ref[...]
    tail[C:] = jnp.zeros((TAIL - C, 128), jnp.float32)
    pack(main, tail, staged)
    total = staged[: LANES * SHARE].reshape(LANES, SHARE, 128) + other_ref[...].astype(jnp.float32)
    shares_ref[...] = total.astype(jnp.bfloat16)


def total_kernel(shares_ref, gradient_ref, tail):
    group = lax.broadcasted_iota(jnp.int32, (3, 128), 1) // 32
    ends = []
    for quarter in range(4):
        for core in range(2):
            acc = None
            for k in range(16):
                y, z, x = quarter // 2 + 2 * (k // 8), quarter % 2 + 2 * (k // 2 % 4), k % 2
                lane = ((y * 8 + z) * 2 + x) * 2 + core
                term = shares_ref[lane].astype(jnp.float32)
                acc = term if acc is None else acc + term
            at = 128 * (2 * quarter + core)
            gradient_ref[:, 0, at : at + 128] = acc[:10]
            ends.append(acc[10:13])
    for block in range(2):
        for q in range(4):
            row = None
            for g in range(4):
                end = ends[4 * block + g]
                end = end if g == q else pltpu.roll(end, (32 * (g - q)) % 128, 1)
                row = end if row is None else jnp.where(group == g, end, row)
            tail[pl.ds(q, 3, 4)] = row
        at = 1024 + 128 * block
        gradient_ref[:, 0, at : at + 128] = tail[:10]


def partner(y, z, core, t):
    y = ((y + core) % 4 ^ 1) - core if t & 2 else y
    z = ((z + core) % 8 ^ 1) - core if t & 1 else z
    return ((y % 4) * 8 + z % 8) * 2 + core


def squares():
    groups = []
    for x in range(2):
        for core in range(2):
            for y in range(0, 4, 2):
                for z in range(0, 8, 2):
                    group = []
                    for section in range(2):
                        for quarter in range(4):
                            near = (y + core + (quarter // 2 + core) % 2) % 4
                            side = (z + core + (quarter % 2 + core) % 2) % 8
                            group.append((((section * 4 + near) * 8 + side) * 2 + x) * 2 + core)
                    groups.append(group)
    return groups


def exchange(block, t, moves):
    at = [(y, z, core) for y in range(4) for z in range(8) for core in range(2)]
    route = [
        (64 * source + partner(*place, 0), 64 * target + partner(*place, t))
        for source, target in moves
        for place in at
    ]
    return lax.ppermute(block, ("section", "y", "z", "core"), route)


def local(inputs, weights, gains, timesteps, text_pooled):
    half = jax.ShapeDtypeStruct((ROWS, C), jnp.bfloat16)
    whole = jax.ShapeDtypeStruct(inputs.shape, jnp.bfloat16)
    sent_0, sent_1, active_0, active_1, condition, weight = pl.pallas_call(
        down_kernel,
        out_shape=(half,) * 4
        + (
            jax.ShapeDtypeStruct((MICRO, 1, C), jnp.float32),
            jax.ShapeDtypeStruct((C, C), jnp.bfloat16),
        ),
        in_specs=[HBM] * 5,
        out_specs=(VMEM,) * 6,
        scratch_shapes=[
            pltpu.SMEM(timesteps.shape, jnp.int32),
            pltpu.VMEM(inputs.shape[1:], jnp.bfloat16),
            pltpu.VMEM(gains.shape, jnp.float32),
            pltpu.VMEM(text_pooled.shape, jnp.bfloat16),
            pltpu.SemaphoreType.DMA((5,)),
        ],
        compiler_params=WHOLE,
    )(timesteps, inputs, weights, gains, text_pooled)
    sent, first_active = (sent_0, sent_1), (active_0, active_1)
    received = [lax.ppermute(rows, "section", [(0, 1)]) for rows in sent]
    both = jax.ShapeDtypeStruct((MICRO * ROWS, C), jnp.bfloat16)
    piece = jax.ShapeDtypeStruct((PIECE, 128), jnp.bfloat16)
    slots = jax.ShapeDtypeStruct((8, PIECE, 128), jnp.bfloat16)

    def up(number, *before):
        return pl.pallas_call(
            functools.partial(up_kernel, number),
            out_shape=(whole, both, half, half),
            in_specs=[VMEM, VMEM, HBM, VMEM, VMEM] + [HBM] * (2 + 2 * number),
            out_specs=(HBM, HBM, VMEM, VMEM),
            scratch_shapes=[
                pltpu.VMEM((ROWS, C), jnp.bfloat16),
                pltpu.VMEM((ROWS, C), jnp.bfloat16),
                pltpu.VMEM((ROWS, C), jnp.bfloat16),
                pltpu.SemaphoreType.DMA((3,)),
            ],
            input_output_aliases={7: 0, 8: 1} if number else {},
            compiler_params=MOST,
            cost_estimate=pl.CostEstimate(
                flops=2_000_000_000, bytes_accessed=4_000_000, transcendentals=0
            ),
        )(
            condition, received[number], inputs, weight, gains, sent[number],
            first_active[number], *before,
        )

    outs, actives, cot_0, back_0 = up(0)
    returned = lax.ppermute(back_0, "section", [(1, 0)])
    outs, actives, cot_1, back_1 = up(1, outs, actives)
    pieces = pl.pallas_call(
        pieces_kernel,
        out_shape=slots,
        in_specs=[VMEM] * 3,
        out_specs=HBM,
        scratch_shapes=[
            pltpu.VMEM((8, PIECE, 128), jnp.bfloat16),
            pltpu.SemaphoreType.DMA((2,)),
        ],
        compiler_params=MOST,
        cost_estimate=pl.CostEstimate(flops=COST, bytes_accessed=2_000_000, transcendentals=0),
    )(returned, cot_1, back_1)
    cots = pl.pallas_call(
        cots_kernel,
        out_shape=(piece,) * 3,
        in_specs=[VMEM, HBM],
        out_specs=(VMEM,) * 3,
        scratch_shapes=[pltpu.VMEM((4, PIECE, 128), jnp.bfloat16)],
        compiler_params=PARAMS,
    )(cot_0, pieces)
    others = [exchange(actives, t, ((0, 0), (1, 1))) for t in range(1, 4)]
    turned = [exchange(cots[t - 1], t, ((1, 1),)) for t in range(1, 4)]
    arrived = lax.all_to_all(
        pieces, ("section",) + DP, 0, 0, axis_index_groups=squares(), tiled=True
    )
    packed = [
        pltpu.VMEM((TAIL, 128), jnp.float32),
        pltpu.VMEM((TAIL, 128), jnp.float32),
        pltpu.VMEM((LANES * SHARE + SHARE, 128), jnp.float32),
    ]
    share = jax.ShapeDtypeStruct((LANES, SHARE, 128), jnp.bfloat16)
    own = pl.pallas_call(
        own_kernel,
        out_shape=piece,
        in_specs=[VMEM] + [HBM] * 3,
        out_specs=VMEM,
        scratch_shapes=[pltpu.VMEM((4, PIECE, 128), jnp.bfloat16)],
        compiler_params=PARAMS,
        cost_estimate=pl.CostEstimate(flops=COST, bytes_accessed=2_000_000, transcendentals=0),
    )(cot_0, *others)
    main, tail, away = pl.pallas_call(
        weight_kernel,
        out_shape=(jax.ShapeDtypeStruct((C, 128), jnp.float32),) * 2 + (share,),
        in_specs=[VMEM] * 9,
        out_specs=(VMEM,) * 3,
        scratch_shapes=packed,
        compiler_params=PARAMS,
    )(actives, *others, arrived, own, *turned)
    other = lax.ppermute(away, "core", [(0, 1), (1, 0)])
    shares = pl.pallas_call(
        pair_kernel,
        out_shape=share,
        in_specs=[VMEM] * 3,
        out_specs=VMEM,
        scratch_shapes=packed,
        compiler_params=PARAMS,
    )(main, tail, other)
    shares = lax.all_to_all(shares, DP, 0, 0, tiled=True)
    gradient = pl.pallas_call(
        total_kernel,
        out_shape=jax.ShapeDtypeStruct((C // LANES, 1, C), jnp.float32),
        in_specs=[VMEM],
        out_specs=VMEM,
        scratch_shapes=[pltpu.VMEM((40, 128), jnp.float32)],
        compiler_params=PARAMS,
    )(shares)
    return (outs, jnp.transpose(gradient, (1, 0, 2)))


def solution(mesh):
    fine = Mesh(mesh.devices.reshape(2, 4, 8, 2, 2), ("section",) + DP)
    return jax.shard_map(
        local,
        mesh=fine,
        in_specs=(
            P("section", None, DP, None),
            P("section", None, None),
            P("section", None),
            P(),
            P(),
        ),
        out_specs=(P("section", None, DP, None), P("section", DP, None)),
        check_vma=False,
    )
```

```python
import functools
import math

import jax
import jax.numpy as jnp
from jax import lax
from jax.experimental import pallas as pl
from jax.experimental.pallas import tpu as pltpu
from jax.sharding import Mesh, PartitionSpec as P

PIX = 1024
MICRO = 2
ROWS = 128
LANES = 128
C = 1280
DP = ("y", "z", "x", "core")
COST = 50_000_000_000
PIECE = 320
SHARE = 16
TAIL = C + 48
PARAMS = pltpu.CompilerParams(vmem_limit_bytes=40 * 1024 * 1024)
WHOLE = pltpu.CompilerParams(vmem_limit_bytes=52 * 1024 * 1024)
MOST = pltpu.CompilerParams(vmem_limit_bytes=51 * 1024 * 1024)
VMEM = pl.BlockSpec(memory_space=pltpu.VMEM)
HBM = pl.BlockSpec(memory_space=pltpu.HBM)


def condition_row(steps_ref, text_ref, number):
    latent = lax.axis_index(DP) * ROWS // PIX
    step = steps_ref[number, latent].astype(jnp.float32)
    lane = lax.broadcasted_iota(jnp.int32, (1, C), 1)
    index = jnp.where(lane < C // 2, lane, lane - C // 2).astype(jnp.float32)
    angle = step * jnp.exp(-math.log(10000.0) * index / (C // 2))
    waves = jnp.where(lane < C // 2, jnp.cos(angle), jnp.sin(angle))
    text = text_ref[number].astype(jnp.float32)
    mine = lax.broadcasted_iota(jnp.int32, text.shape, 0) == latent
    return waves + jnp.sum(jnp.where(mine, text, 0.0), axis=0, keepdims=True)


def normed_rows(hidden, condition, gain):
    shifted = hidden + condition
    inverse = lax.rsqrt(jnp.mean(shifted * shifted, axis=-1, keepdims=True) + 1e-05)
    normed = shifted * inverse * gain
    sigma = 1.0 / (1.0 + jnp.exp(-normed))
    return shifted, inverse, normed, sigma


def down_kernel(
    steps_hbm, rows_hbm, weight_hbm, gain_hbm, text_hbm,
    sent_0, sent_1, active_0, active_1, cond_ref, weight_ref,
    steps_ref, rows_ref, gain_ref, text_ref, sems,
):
    copies = [
        pltpu.make_async_copy(source, target, sems.at[at])
        for at, (source, target) in enumerate(
            (
                (steps_hbm, steps_ref),
                (text_hbm, text_ref),
                (rows_hbm.at[0], rows_ref),
                (gain_hbm, gain_ref),
                (weight_hbm.at[0], weight_ref),
            )
        )
    ]
    for at in (0, 4, 1, 2, 3):
        copies[at].start()
    copies[0].wait()
    copies[1].wait()
    for number in range(MICRO):
        cond_ref[number] = condition_row(steps_ref, text_ref, number)
    copies[2].wait()
    copies[3].wait()
    for number, sent_ref, active_ref in ((0, sent_0, active_0), (1, sent_1, active_1)):
        hidden = rows_ref[number].astype(jnp.float32)
        _, _, normed, sigma = normed_rows(hidden, cond_ref[number], gain_ref[...])
        active = (normed * sigma).astype(jnp.bfloat16)
        active_ref[...] = active
        if number == 0:
            copies[4].wait()
        result = hidden + jnp.dot(active, weight_ref[...], preferred_element_type=jnp.float32)
        sent_ref[...] = result.astype(jnp.bfloat16)


def own_quarter():
    return 2 * lax.rem(lax.axis_index("y"), 2) + lax.rem(lax.axis_index("z"), 2)


def store_pieces(pieces_ref, first, values):
    half = ROWS // 2
    low = lax.broadcasted_iota(jnp.int32, (half, 128), 1) < 64
    rounded = values.astype(jnp.bfloat16)
    for quarter in range(4):
        slot = first + quarter
        pieces_ref[slot, :ROWS] = rounded[:, 256 * quarter : 256 * quarter + 128]
        pieces_ref[slot, ROWS : 2 * ROWS] = rounded[:, 256 * quarter + 128 : 256 * quarter + 256]
        at = 1024 + 128 * (quarter // 2)
        block = values[:, at : at + 128]
        turned = pltpu.roll(block, 64, 1)
        top, bottom = (block, turned) if quarter % 2 == 0 else (turned, block)
        pieces_ref[slot, 2 * ROWS :] = jnp.where(low, top[:half], bottom[half:]).astype(
            jnp.bfloat16
        )


def up_kernel(number, *refs):
    cond_ref, arrived_ref, rows_hbm, weight_ref, gain_ref, sent_hbm, first_active_hbm = refs[:7]
    outs_hbm, actives_hbm, cot_ref, back_ref = refs[7 + 2 * number : -4]
    out_ref, active_ref, rows_ref, sems = refs[-4:]
    active_hbm = actives_hbm.at[pl.ds(ROWS * number, ROWS)]
    rows_copy = pltpu.make_async_copy(rows_hbm.at[0, number], rows_ref, sems.at[0])
    rows_copy.start()
    down = lax.axis_index("section") == 0
    kept = [
        pltpu.make_async_copy(sent_hbm, outs_hbm.at[0, number], sems.at[1]),
        pltpu.make_async_copy(first_active_hbm, active_hbm, sems.at[2]),
    ]
    made = [
        pltpu.make_async_copy(out_ref, outs_hbm.at[0, number], sems.at[1]),
        pltpu.make_async_copy(active_ref, active_hbm, sems.at[2]),
    ]

    @pl.when(down)
    def _():
        for copy in kept:
            copy.start()

    gain = gain_ref[...]
    hidden = arrived_ref[...].astype(jnp.float32)
    shifted, inverse, normed, sigma = normed_rows(hidden, cond_ref[number], gain)
    active = (normed * sigma).astype(jnp.bfloat16)
    active_ref[...] = active
    weight = weight_ref[...]
    upper = hidden + jnp.dot(active, weight, preferred_element_type=jnp.float32)
    out_ref[...] = upper.astype(jnp.bfloat16)

    @pl.when(jnp.logical_not(down))
    def _():
        for copy in made:
            copy.start()

    rows_copy.wait()
    cot = (upper - rows_ref[...].astype(jnp.float32)) / math.sqrt(MICRO * ROWS * LANES)
    cot = cot.astype(jnp.bfloat16)
    cot_ref[...] = cot
    through = lax.dot_general(
        cot, weight, (((1,), (1,)), ((), ())), preferred_element_type=jnp.float32
    )
    scaled = through * sigma * (1.0 + normed * (1.0 - sigma)) * gain
    inner = jnp.mean(scaled * shifted, axis=-1, keepdims=True)
    back = cot.astype(jnp.float32) + inverse * scaled - shifted * inverse**3 * inner
    back_ref[...] = back.astype(jnp.bfloat16)

    @pl.when(down)
    def _():
        for copy in kept:
            copy.wait()

    @pl.when(jnp.logical_not(down))
    def _():
        for copy in made:
            copy.wait()


def pack(main, tail, staged):
    group = lax.broadcasted_iota(jnp.int32, (3, 128), 1) // 32
    staged[...] = jnp.zeros_like(staged)

    def lanes(block, carry):
        base = pl.multiple_of(block * 80, 80)
        to = pl.multiple_of(block * 8 * SHARE, 8 * SHARE)
        for lane in range(8):
            at, put = base + 10 * lane, to + SHARE * lane
            staged[pl.ds(put, 10)] = main[pl.ds(at, 10)]
            row = tail[pl.ds(at, 3, 4)]
            for q in range(1, 4):
                row = jnp.where(group == q, tail[pl.ds(at + q, 3, 4)], row)
            staged[pl.ds(put + 10, 3)] = row
        return carry

    lax.fori_loop(0, LANES // 8, lanes, 0)


def pieces_kernel(returned_ref, cot_ref, back_ref, pieces_hbm, pieces_ref, sems):
    copies = [
        pltpu.make_async_copy(pieces_ref.at[pl.ds(at, 4)], pieces_hbm.at[pl.ds(at, 4)], sem)
        for at, sem in ((0, sems.at[0]), (4, sems.at[1]))
    ]
    store_pieces(pieces_ref, 4, cot_ref[...].astype(jnp.float32))
    copies[1].start()
    down = lax.axis_index("section") == 0
    rows = jnp.where(down, returned_ref[...], back_ref[...])
    store_pieces(pieces_ref, 0, rows.astype(jnp.float32))
    copies[0].start()
    for copy in copies:
        copy.wait()


def cots_kernel(cot_ref, pieces_hbm, *refs):
    del pieces_hbm
    store_pieces(refs[3], 0, cot_ref[...].astype(jnp.float32))
    own = own_quarter()
    for turn in range(1, 4):
        refs[turn - 1][...] = refs[3][lax.bitwise_xor(own, turn)]


def gathered_kernel(*refs):
    refs[-1][...] = jnp.zeros_like(refs[-1])


def weight_kernel(*refs):
    active_refs, piece_ref, cot_ref, cot_refs = refs[:4], refs[4], refs[5], refs[6:9]
    main_ref, tail_ref, away_ref, main, tail, staged, own_ref = refs[10:]
    down, core = lax.axis_index("section") == 0, lax.axis_index("core")
    own = own_quarter()
    store_pieces(own_ref, 0, cot_ref[...].astype(jnp.float32))
    low = lax.broadcasted_iota(jnp.int32, (ROWS // 2, 128), 1) < 64
    zero = jnp.zeros((ROWS // 2, 128), jnp.bfloat16)
    product = None
    for turn in range(4):
        right = []
        for number in range(MICRO):
            piece = piece_ref[4 * number + lax.bitwise_xor(own, turn)]
            if number == 0:
                cot = cot_refs[turn - 1][...] if turn else own_ref[own]
                piece = jnp.where(down, piece, cot)
            end = piece[2 * ROWS :]
            right.append(
                jnp.concatenate(
                    [
                        piece[:ROWS],
                        piece[ROWS : 2 * ROWS],
                        jnp.concatenate([jnp.where(low, end, zero), jnp.where(low, zero, end)]),
                    ],
                    axis=1,
                )
            )
        term = lax.dot_general(
            active_refs[turn][...], jnp.concatenate(right), (((0,), (0,)), ((), ())),
            preferred_element_type=jnp.float32,
        )
        product = term if product is None else product + term
    first, second = product[:, :128], product[:, 128:256]
    both = product[:, 256:] + pltpu.roll(product[:, 256:], 64, 1)
    turned = pltpu.roll(both, 32, 1)
    even = (lax.broadcasted_iota(jnp.int32, both.shape, 1) // 32) % 2 == 0
    lower, upper = jnp.where(even, both, turned), jnp.where(even, turned, both)
    zeroth = core == 0
    main_ref[...] = jnp.where(zeroth, first, second)
    tail_ref[...] = jnp.where(zeroth, lower, upper)
    main[:C] = jnp.where(zeroth, second, first)
    tail[:C] = jnp.where(zeroth, upper, lower)
    tail[C:] = jnp.zeros((TAIL - C, 128), jnp.float32)
    pack(main, tail, staged)
    away_ref[...] = staged[: LANES * SHARE].astype(jnp.bfloat16).reshape(LANES, SHARE, 128)


def pair_kernel(main_ref, tail_ref, other_ref, shares_ref, main, tail, staged):
    main[:C] = main_ref[...]
    tail[:C] = tail_ref[...]
    tail[C:] = jnp.zeros((TAIL - C, 128), jnp.float32)
    pack(main, tail, staged)
    total = staged[: LANES * SHARE].reshape(LANES, SHARE, 128) + other_ref[...].astype(jnp.float32)
    shares_ref[...] = total.astype(jnp.bfloat16)


def total_kernel(shares_ref, gradient_ref, tail):
    group = lax.broadcasted_iota(jnp.int32, (3, 128), 1) // 32
    ends = []
    for quarter in range(4):
        for core in range(2):
            acc = None
            for k in range(16):
                y, z, x = quarter // 2 + 2 * (k // 8), quarter % 2 + 2 * (k // 2 % 4), k % 2
                lane = ((y * 8 + z) * 2 + x) * 2 + core
                term = shares_ref[lane].astype(jnp.float32)
                acc = term if acc is None else acc + term
            at = 128 * (2 * quarter + core)
            gradient_ref[:, 0, at : at + 128] = acc[:10]
            ends.append(acc[10:13])
    for block in range(2):
        for q in range(4):
            row = None
            for g in range(4):
                end = ends[4 * block + g]
                end = end if g == q else pltpu.roll(end, (32 * (g - q)) % 128, 1)
                row = end if row is None else jnp.where(group == g, end, row)
            tail[pl.ds(q, 3, 4)] = row
        at = 1024 + 128 * block
        gradient_ref[:, 0, at : at + 128] = tail[:10]


def partner(y, z, core, t):
    y = ((y + core) % 4 ^ 1) - core if t & 2 else y
    z = ((z + core) % 8 ^ 1) - core if t & 1 else z
    return ((y % 4) * 8 + z % 8) * 2 + core


def squares():
    groups = []
    for x in range(2):
        for core in range(2):
            for y in range(0, 4, 2):
                for z in range(0, 8, 2):
                    group = []
                    for section in range(2):
                        for quarter in range(4):
                            near = (y + core + (quarter // 2 + core) % 2) % 4
                            side = (z + core + (quarter % 2 + core) % 2) % 8
                            group.append((((section * 4 + near) * 8 + side) * 2 + x) * 2 + core)
                    groups.append(group)
    return groups


def exchange(block, t, moves):
    at = [(y, z, core) for y in range(4) for z in range(8) for core in range(2)]
    route = [
        (64 * source + partner(*place, 0), 64 * target + partner(*place, t))
        for source, target in moves
        for place in at
    ]
    return lax.ppermute(block, ("section", "y", "z", "core"), route)


def local(inputs, weights, gains, timesteps, text_pooled):
    half = jax.ShapeDtypeStruct((ROWS, C), jnp.bfloat16)
    whole = jax.ShapeDtypeStruct(inputs.shape, jnp.bfloat16)
    sent_0, sent_1, active_0, active_1, condition, weight = pl.pallas_call(
        down_kernel,
        out_shape=(half,) * 4
        + (
            jax.ShapeDtypeStruct((MICRO, 1, C), jnp.float32),
            jax.ShapeDtypeStruct((C, C), jnp.bfloat16),
        ),
        in_specs=[HBM] * 5,
        out_specs=(VMEM,) * 6,
        scratch_shapes=[
            pltpu.SMEM(timesteps.shape, jnp.int32),
            pltpu.VMEM(inputs.shape[1:], jnp.bfloat16),
            pltpu.VMEM(gains.shape, jnp.float32),
            pltpu.VMEM(text_pooled.shape, jnp.bfloat16),
            pltpu.SemaphoreType.DMA((5,)),
        ],
        compiler_params=WHOLE,
    )(timesteps, inputs, weights, gains, text_pooled)
    sent, first_active = (sent_0, sent_1), (active_0, active_1)
    received = [lax.ppermute(rows, "section", [(0, 1)]) for rows in sent]
    both = jax.ShapeDtypeStruct((MICRO * ROWS, C), jnp.bfloat16)
    piece = jax.ShapeDtypeStruct((PIECE, 128), jnp.bfloat16)
    slots = jax.ShapeDtypeStruct((8, PIECE, 128), jnp.bfloat16)

    def up(number, *before):
        return pl.pallas_call(
            functools.partial(up_kernel, number),
            out_shape=(whole, both, half, half),
            in_specs=[VMEM, VMEM, HBM, VMEM, VMEM] + [HBM] * (2 + 2 * number),
            out_specs=(HBM, HBM, VMEM, VMEM),
            scratch_shapes=[
                pltpu.VMEM((ROWS, C), jnp.bfloat16),
                pltpu.VMEM((ROWS, C), jnp.bfloat16),
                pltpu.VMEM((ROWS, C), jnp.bfloat16),
                pltpu.SemaphoreType.DMA((3,)),
            ],
            input_output_aliases={7: 0, 8: 1} if number else {},
            compiler_params=MOST,
            cost_estimate=pl.CostEstimate(
                flops=2_000_000_000, bytes_accessed=4_000_000, transcendentals=0
            ),
        )(
            condition, received[number], inputs, weight, gains, sent[number],
            first_active[number], *before,
        )

    outs, actives, cot_0, back_0 = up(0)
    returned = lax.ppermute(back_0, "section", [(1, 0)])
    outs, actives, cot_1, back_1 = up(1, outs, actives)
    pieces = pl.pallas_call(
        pieces_kernel,
        out_shape=slots,
        in_specs=[VMEM] * 3,
        out_specs=HBM,
        scratch_shapes=[
            pltpu.VMEM((8, PIECE, 128), jnp.bfloat16),
            pltpu.SemaphoreType.DMA((2,)),
        ],
        compiler_params=MOST,
        cost_estimate=pl.CostEstimate(flops=COST, bytes_accessed=2_000_000, transcendentals=0),
    )(returned, cot_1, back_1)
    cots = pl.pallas_call(
        cots_kernel,
        out_shape=(piece,) * 3,
        in_specs=[VMEM, HBM],
        out_specs=(VMEM,) * 3,
        scratch_shapes=[pltpu.VMEM((4, PIECE, 128), jnp.bfloat16)],
        compiler_params=PARAMS,
    )(cot_0, pieces)
    others = [exchange(actives, t, ((0, 0), (1, 1))) for t in range(1, 4)]
    turned = [exchange(cots[t - 1], t, ((1, 1),)) for t in range(1, 4)]
    arrived = lax.all_to_all(
        pieces, ("section",) + DP, 0, 0, axis_index_groups=squares(), tiled=True
    )
    packed = [
        pltpu.VMEM((TAIL, 128), jnp.float32),
        pltpu.VMEM((TAIL, 128), jnp.float32),
        pltpu.VMEM((LANES * SHARE + SHARE, 128), jnp.float32),
    ]
    share = jax.ShapeDtypeStruct((LANES, SHARE, 128), jnp.bfloat16)
    gathered = pl.pallas_call(
        gathered_kernel,
        out_shape=jax.ShapeDtypeStruct((8, 128), jnp.float32),
        in_specs=[HBM] * 3,
        out_specs=VMEM,
        compiler_params=PARAMS,
        cost_estimate=pl.CostEstimate(flops=COST, bytes_accessed=2_000_000, transcendentals=0),
    )(*others)
    main, tail, away = pl.pallas_call(
        weight_kernel,
        out_shape=(jax.ShapeDtypeStruct((C, 128), jnp.float32),) * 2 + (share,),
        in_specs=[VMEM] * 9 + [HBM],
        out_specs=(VMEM,) * 3,
        scratch_shapes=packed + [pltpu.VMEM((4, PIECE, 128), jnp.bfloat16)],
        compiler_params=PARAMS,
    )(actives, *others, arrived, cot_0, *turned, gathered)
    other = lax.ppermute(away, "core", [(0, 1), (1, 0)])
    shares = pl.pallas_call(
        pair_kernel,
        out_shape=share,
        in_specs=[VMEM] * 3,
        out_specs=VMEM,
        scratch_shapes=packed,
        compiler_params=PARAMS,
    )(main, tail, other)
    shares = lax.all_to_all(shares, DP, 0, 0, tiled=True)
    gradient = pl.pallas_call(
        total_kernel,
        out_shape=jax.ShapeDtypeStruct((C // LANES, 1, C), jnp.float32),
        in_specs=[VMEM],
        out_specs=VMEM,
        scratch_shapes=[pltpu.VMEM((40, 128), jnp.float32)],
        compiler_params=PARAMS,
    )(shares)
    return (outs, jnp.transpose(gradient, (1, 0, 2)))


def solution(mesh):
    fine = Mesh(mesh.devices.reshape(2, 4, 8, 2, 2), ("section",) + DP)
    return jax.shard_map(
        local,
        mesh=fine,
        in_specs=(
            P("section", None, DP, None),
            P("section", None, None),
            P("section", None),
            P(),
            P(),
        ),
        out_specs=(P("section", None, DP, None), P("section", DP, None)),
        check_vma=False,
    )
```
